32 devices in a mesh: chan: 8 (over y, x, core), hour: 4 (over z).
Axes of the slice: x: 2, y: 2, z: 4, core: 2. Of those that a mesh axis runs over, the one named last changes fastest.
Arguments:
- spectra: bfloat16 [2, 64, 800, 1024], P(None, 'hour', None, 'chan'), may hold values from -6 to 6
- quality: int32 [64, 1024], P('hour', 'chan'), may hold values 0 or 1
- sources: int32 [32], replicated, may hold values from 0 to 1023
Outputs:
- correlation: bfloat16 [32, 512, 1024], P('hour', None, 'chan')
The draws below stay inside these ranges and needn't reach their ends.
Inputs may be any that keep to these rules, and one draw needn't show every extreme that they name: `sources`: indices may repeat.
All inputs are finite; a program needn't handle non-finite values. No bound on the sum of `quality` on one device may be relied on, other than what follows from the above.
Results may differ from the reference program's by a relative error of at most 0.01.
Values may be sent and summed in bfloat16 or wider, within the bound.
No kernel may reach another device: no remote copies, remote signals or barrier semaphores. Data moves between devices by JAX's collectives and lax.ppermute only.
A program may use at most 128 MiB of HBM per device.

```python
import math
import jax
import jax.numpy as jnp
from jax import lax

C_DEV = 128
W_DEV = 16
F_BINS = 800
LAGS = 512
S_SRC = 32
CHANNELS = 1024
WINDOWS = 64
N_HOUR = 4


def with_ends(result, rng, low, high):
    dims = result.shape
    index_at = [jax.random.randint(jax.random.fold_in(rng, axis), (), 0, dims[axis]) for axis in range(len(dims))]
    result = result.at[tuple(index_at)].set(low)
    longest = dims.index(max(dims))
    index_at[longest] = (index_at[longest] + 1) % dims[longest]
    return result.at[tuple(index_at)].set(high)


def level_of(rng, shape, split, low, top_value):
    def one(position, shards_of):
        steps = jax.random.uniform(jax.random.fold_in(jax.random.fold_in(rng, 6), position), (shards_of,), jnp.float32, low / len(split), top_value / len(split))
        return jnp.repeat(jnp.exp(steps), shape[position] // shards_of).reshape((-1,) + (1,) * (len(shape) - position - 1))

    loudness = one(*split[0])
    for cut in split[1:]:
        loudness = loudness * one(*cut)
    return loudness


def centred(stream_key, extent, deviation, most, split=(), kind=jnp.bfloat16):
    result = deviation * jax.random.normal(stream_key, extent, jnp.float32)
    if split:
        result = result * level_of(stream_key, extent, split, -0.22, 0.18)
    return jnp.clip(result, -most, most).astype(kind)


def setup_inputs(seed: int = 0) -> dict:
    streams_of = jax.random.split(jax.random.key(seed), 4)
    spectra = centred(streams_of[0], (2, WINDOWS, F_BINS, CHANNELS), 1.0, 6.0, ((1, 4), (3, 8)))
    quality = with_ends((jax.random.randint(streams_of[1], (WINDOWS, CHANNELS), 0, 4) < 3).astype(jnp.int32), jax.random.fold_in(streams_of[1], 1), 0, 1)
    sources = with_ends(jax.random.randint(streams_of[2], (S_SRC,), 0, CHANNELS), jax.random.fold_in(streams_of[2], 1), 0, CHANNELS - 1).astype(jnp.int32)
    return dict(spectra=spectra, quality=quality, sources=sources)


def whiten(record, usable):
    as_float = record.astype(jnp.float32)
    power = lax.optimization_barrier(jnp.mean(as_float[0] * as_float[0] + as_float[1] * as_float[1], axis=1))
    scale = lax.rsqrt(power + 1e-06) * usable.astype(jnp.float32)
    return (as_float * scale[None, :, None, :]).astype(jnp.bfloat16)

def lag_table(freq_count, lag_count):
    bin_number = jnp.arange(freq_count, dtype=jnp.float32) + 1.0
    lag_offset = jnp.arange(lag_count, dtype=jnp.float32) - float(lag_count // 2)
    phase = math.pi * bin_number[:, None] * lag_offset[None, :] / freq_count
    return (jnp.stack([jnp.cos(phase), -jnp.sin(phase)]) / freq_count).astype(jnp.bfloat16)

def cross_spectrum(source_spec, receivers):
    left_real = source_spec.astype(jnp.float32)
    right_real = receivers.astype(jnp.float32)
    real_part = jnp.einsum('kwfs,kwfc->fsc', left_real, right_real)
    left_pair = jnp.stack([left_real[0], -left_real[1]])
    right_pair = jnp.stack([right_real[1], right_real[0]])
    imag_part = jnp.einsum('kwfs,kwfc->fsc', left_pair, right_pair)
    return jnp.stack([real_part, imag_part]).astype(jnp.bfloat16)

def reference(spectra, quality, sources):
    source_spec = whiten(spectra[:, :, :, sources], quality[:, sources])
    table = lag_table(F_BINS, LAGS).astype(jnp.float32)

    def one_block(block_id):
        first = (block_id * C_DEV).astype(jnp.int32)
        raw = lax.dynamic_slice_in_dim(spectra, first, C_DEV, 3)
        usable = lax.dynamic_slice_in_dim(quality, first, C_DEV, 1)
        receivers = whiten(raw, usable)
        total = jnp.zeros((S_SRC, LAGS, C_DEV), jnp.float32)
        for hour_id in range(N_HOUR):
            low = hour_id * W_DEV
            partial_value = cross_spectrum(source_spec[:, low:low + W_DEV], receivers[:, low:low + W_DEV])
            total = total + jnp.einsum('kfsc,kfl->slc', partial_value.astype(jnp.float32), table)
        return total.astype(jnp.bfloat16)
    blocks = lax.map(one_block, jnp.arange(CHANNELS // C_DEV, dtype=jnp.int32))
    return blocks.transpose(1, 2, 0, 3).reshape(S_SRC, LAGS, CHANNELS)
```

```python
import functools
import math

import jax
import jax.numpy as jnp
from jax import lax
from jax.experimental import pallas as pl
from jax.experimental.pallas import tpu as pltpu
from jax.sharding import PartitionSpec as P

LAGS = 512
GROUP = 16
STEP_BINS = 160
ORDER = ((3, 2, 1, 0), (3, 2, 0, 1), (0, 1, 3, 2), (0, 1, 2, 3))
INWARD = ((0, 1), (3, 2))
MIDDLE = ((1, 2), (2, 1))
OUTWARD = ((1, 0), (2, 3))
VMEM_LIMIT = 40 * 1024 * 1024


def quarter_of(hour, slot):
    quarter = jnp.int32(ORDER[0][slot])
    for row in range(1, 4):
        quarter = jnp.where(hour == row, jnp.int32(ORDER[row][slot]), quarter)
    return quarter


def pick_kernel(sources_ref, spectra_ref, quality_ref, *refs):
    out_refs, (onehot_ref, usable_ref) = refs[:-2], refs[-2:]
    source_count = onehot_ref.shape[0]
    per_slot = source_count // 4
    window_count, channels_here = quality_ref.shape
    wide = window_count * GROUP
    chan = lax.axis_index("chan")

    @pl.when(pl.program_id(0) == 0)
    def _():
        hour = lax.axis_index("hour")
        row = lax.broadcasted_iota(jnp.int32, (source_count, channels_here), 0)
        lane = lax.broadcasted_iota(jnp.int32, (source_count, channels_here), 1)
        wanted = jnp.full((source_count, channels_here), -1, jnp.int32)
        for slot in range(4):
            first = quarter_of(hour, slot) * per_slot
            for at in range(per_slot):
                wanted = jnp.where(row == slot * per_slot + at, sources_ref[first + at], wanted)
        onehot = (wanted - chan * channels_here == lane).astype(jnp.float32).astype(jnp.bfloat16)
        onehot_ref[...] = onehot
        usable = lax.dot_general(
            onehot,
            quality_ref[...].astype(jnp.float32).astype(jnp.bfloat16),
            (((1,), (1,)), ((), ())),
            preferred_element_type=jnp.float32,
        )
        spread = (
            lax.broadcasted_iota(jnp.int32, (window_count, wide), 1) // GROUP
            == lax.broadcasted_iota(jnp.int32, (window_count, wide), 0)
        )
        usable_ref[...] = jnp.dot(
            usable.astype(jnp.bfloat16),
            spread.astype(jnp.float32).astype(jnp.bfloat16),
            preferred_element_type=jnp.float32,
        )

    even = (chan % 2) == 0
    onehot = onehot_ref[...]
    usable = usable_ref[...]
    own, other = [], []
    for group in range(spectra_ref.shape[2] // GROUP):
        picked = []
        for part in range(2):
            columns = spectra_ref[part, :, group * GROUP : (group + 1) * GROUP, :]
            columns = columns.reshape(wide, channels_here)
            picked.append(
                lax.dot_general(
                    onehot, columns, (((1,), (1,)), ((), ())), preferred_element_type=jnp.float32
                )
                * usable
            )
        own.append(jnp.where(even, picked[0], picked[1]))
        other.append(jnp.where(even, picked[1], picked[0]))
    for slot in range(4):
        rows = slice(slot * per_slot, (slot + 1) * per_slot)
        out_refs[slot][...] = jnp.concatenate([v[rows] for v in own], 0).astype(jnp.bfloat16)
        out_refs[4 + slot][...] = jnp.concatenate([v[rows] for v in other], 0).astype(jnp.bfloat16)


def pick(spectra, quality, sources):
    _, window_count, freq_count, channels_here = spectra.shape
    source_count = sources.shape[0]
    per_slot = source_count // 4
    rows = freq_count // GROUP * per_slot
    step_rows = STEP_BINS // GROUP * per_slot
    wide = window_count * GROUP
    return pl.pallas_call(
        pick_kernel,
        grid=(freq_count // STEP_BINS,),
        in_specs=[
            pl.BlockSpec(memory_space=pltpu.SMEM),
            pl.BlockSpec((2, window_count, STEP_BINS, channels_here), lambda i: (0, 0, i, 0)),
            pl.BlockSpec((window_count, channels_here), lambda i: (0, 0)),
        ],
        out_specs=[pl.BlockSpec((step_rows, wide), lambda i: (i, 0))] * 8,
        out_shape=[jax.ShapeDtypeStruct((rows, wide), jnp.bfloat16)] * 8,
        scratch_shapes=[
            pltpu.VMEM((source_count, channels_here), jnp.bfloat16),
            pltpu.VMEM((source_count, wide), jnp.float32),
        ],
        compiler_params=pltpu.CompilerParams(vmem_limit_bytes=VMEM_LIMIT),
        cost_estimate=pl.CostEstimate(
            flops=2 * spectra.size * 256, bytes_accessed=spectra.size * 2, transcendentals=0
        ),
        name="pick_sources",
    )(sources, spectra, quality)


def whiten_kernel(spectra_ref, quality_ref, out_ref):
    _, windows, freq_count, channels_here = spectra_ref.shape
    chunk = 80

    for window in range(windows):

        def add(i, total):
            rows = pl.ds(pl.multiple_of(i * chunk, chunk), chunk)
            real = spectra_ref[0, window, rows, :].astype(jnp.float32)
            imag = spectra_ref[1, window, rows, :].astype(jnp.float32)
            square = real * real + imag * imag
            return total + jnp.sum(square.reshape(chunk // 8, 8, channels_here), axis=0)

        total = lax.fori_loop(0, freq_count // chunk, add, jnp.zeros((8, channels_here), jnp.float32))
        power = jnp.sum(total, axis=0, keepdims=True) / freq_count
        usable = quality_ref[pl.ds(pl.program_id(0) * windows + window, 1), :].astype(jnp.float32)
        scale = lax.rsqrt(power + 1e-06) * usable

        def apply(i, carry):
            rows = pl.ds(pl.multiple_of(i * chunk, chunk), chunk)
            for part in range(2):
                value = spectra_ref[part, window, rows, :].astype(jnp.float32) * scale
                out_ref[part, window, rows, :] = value.astype(jnp.bfloat16)
            return carry

        lax.fori_loop(0, freq_count // chunk, apply, 0)


def whiten(spectra, quality):
    _, window_count, freq_count, channels_here = spectra.shape
    windows = 2
    block = pl.BlockSpec((2, windows, freq_count, channels_here), lambda i: (0, i, 0, 0))
    return pl.pallas_call(
        whiten_kernel,
        grid=(window_count // windows,),
        in_specs=[block, pl.BlockSpec((window_count, channels_here), lambda i: (0, 0))],
        out_specs=block,
        out_shape=jax.ShapeDtypeStruct(spectra.shape, jnp.bfloat16),
        compiler_params=pltpu.CompilerParams(vmem_limit_bytes=VMEM_LIMIT),
        cost_estimate=pl.CostEstimate(
            flops=6 * spectra.size, bytes_accessed=spectra.size * 4, transcendentals=0
        ),
        name="whiten_receivers",
    )(spectra, quality)


def lags_kernel(first, count, own_ref, other_ref, receivers_ref, table_ref, out_ref, spec_ref, cross_ref):
    step = pl.program_id(0)
    freq_count = table_ref.shape[1] // 2
    _, window_count, step_bins, channels_here = receivers_ref.shape
    wide = own_ref.shape[1]
    groups = own_ref.shape[0] // 8
    chan = lax.axis_index("chan")

    @pl.when(step == 0)
    def _():
        even = (chan % 2) == 0

        def load(i):
            rows = pl.ds(pl.multiple_of(i * 16, 16), 16)
            own = own_ref[rows, :].astype(jnp.float32)
            other = other_ref[rows, :].astype(jnp.float32)
            return jnp.where(even, own, other), jnp.where(even, other, own)

        def add(i, total):
            real, imag = load(i)
            square = real * real + imag * imag
            return total + square[:8] + square[8:]

        total = lax.fori_loop(0, groups // 2, add, jnp.zeros((8, wide), jnp.float32))
        same = (
            lax.broadcasted_iota(jnp.int32, (wide, wide), 0) // GROUP
            == lax.broadcasted_iota(jnp.int32, (wide, wide), 1) // GROUP
        ).astype(jnp.float32)
        power = jnp.dot(
            total, same, preferred_element_type=jnp.float32, precision=lax.Precision.HIGHEST
        )
        scale = lax.rsqrt(power / freq_count + 1e-06)
        scale = jnp.concatenate([scale, scale], 0)

        def apply(i, carry):
            rows = pl.ds(pl.multiple_of(i * 16, 16), 16)
            for part, value in enumerate(load(i)):
                spec_ref[part, rows, :] = (value * scale).astype(jnp.bfloat16).astype(jnp.float32)
            return carry

        lax.fori_loop(0, groups // 2, apply, 0)

    diagonal = [
        lax.broadcasted_iota(jnp.int32, (8, wide), 1) % GROUP
        == lax.broadcasted_iota(jnp.int32, (8, wide), 0) + low
        for low in (0, 8)
    ]
    zero = jnp.zeros((8, wide), jnp.float32)
    step_groups = step_bins // GROUP
    for group in range(step_groups):
        left = []
        for part in range(2):
            rows = spec_ref[part, pl.ds(pl.multiple_of((step * step_groups + group) * 8, 8), 8), :]
            tiles = []
            for at in range(count):
                row = jnp.broadcast_to(rows[first + at : first + at + 1, :], (8, wide))
                tiles += [jnp.where(mask, row, zero) for mask in diagonal]
            left.append(jnp.concatenate(tiles, 0).astype(jnp.bfloat16))
        bins = slice(group * GROUP, (group + 1) * GROUP)
        real = receivers_ref[0, :, bins, :].reshape(wide, channels_here)
        imag = receivers_ref[1, :, bins, :].reshape(wide, channels_here)
        cross = jnp.dot(
            left[0], jnp.concatenate([real, imag], 1), preferred_element_type=jnp.float32
        ) + jnp.dot(left[1], jnp.concatenate([imag, -real], 1), preferred_element_type=jnp.float32)
        cross = cross.astype(jnp.bfloat16)
        for at in range(count):
            for part in range(2):
                rows = pl.ds(
                    pl.multiple_of(part * freq_count + step * step_bins + group * GROUP, GROUP), GROUP
                )
                cross_ref[at // 2, rows, (at % 2) * channels_here : (at % 2 + 1) * channels_here] = cross[
                    at * GROUP : (at + 1) * GROUP, part * channels_here : (part + 1) * channels_here
                ]

    @pl.when(step == pl.num_programs(0) - 1)
    def _():
        rows = 128
        for pair in range(count // 2):
            for block in range(table_ref.shape[0] // rows):
                lags = slice(block * rows, (block + 1) * rows)
                value = jnp.dot(
                    table_ref[lags, :], cross_ref[pair], preferred_element_type=jnp.float32
                ).astype(jnp.bfloat16)
                out_ref[2 * pair, lags, :] = value[:, :channels_here]
                out_ref[2 * pair + 1, lags, :] = value[:, channels_here:]


def lags_of(own, other, receivers, table, first, count):
    _, window_count, freq_count, channels_here = receivers.shape
    lag_count = table.shape[0]
    rows, wide = own.shape
    whole = lambda shape: pl.BlockSpec(shape, lambda i: (0,) * len(shape))
    return pl.pallas_call(
        functools.partial(lags_kernel, first, count),
        grid=(freq_count // STEP_BINS,),
        in_specs=[
            whole((rows, wide)),
            whole((rows, wide)),
            pl.BlockSpec((2, window_count, STEP_BINS, channels_here), lambda i: (0, 0, i, 0)),
            whole(table.shape),
        ],
        out_specs=whole((count, lag_count, channels_here)),
        out_shape=jax.ShapeDtypeStruct((count, lag_count, channels_here), jnp.bfloat16),
        scratch_shapes=[
            pltpu.VMEM((2, rows, wide), jnp.float32),
            pltpu.VMEM((count // 2, 2 * freq_count, 2 * channels_here), jnp.bfloat16),
        ],
        compiler_params=pltpu.CompilerParams(vmem_limit_bytes=VMEM_LIMIT),
        cost_estimate=pl.CostEstimate(
            flops=count * 16 * 2 * receivers.size * 4, bytes_accessed=receivers.size * 2, transcendentals=0
        ),
        name="lags",
    )(own, other, receivers, table)


def lag_table(freq_count, lag_count):
    lag = lax.broadcasted_iota(jnp.int32, (lag_count, 2 * freq_count), 0) - lag_count // 2
    column = lax.broadcasted_iota(jnp.int32, (lag_count, 2 * freq_count), 1)
    part = (column >= freq_count).astype(jnp.int32)
    turns = (column - part * freq_count + 1) * lag + part * (freq_count // 2)
    turns = lax.rem(lax.rem(turns, 2 * freq_count) + 2 * freq_count, 2 * freq_count)
    return (jnp.cos(turns.astype(jnp.float32) * (math.pi / freq_count)) / freq_count).astype(jnp.bfloat16)


def sum_over_chan(own, other, chan_count):
    bits = [1 << b for b in range(1, chan_count.bit_length() - 1)]
    turned = bits[1:] + bits[:1]
    swap = [(i, i ^ 1) for i in range(chan_count)]
    own = own + lax.ppermute(other, "chan", swap)
    for even_bit, odd_bit in zip(bits, turned):
        pairs = [(i, i ^ (odd_bit if i % 2 else even_bit)) for i in range(chan_count)]
        own = own + lax.ppermute(own, "chan", pairs)
    return own, lax.ppermute(own, "chan", swap)


def add(*values):
    return sum(v.astype(jnp.float32) for v in values).astype(jnp.bfloat16)


def body(chan_count, spectra, quality, sources):
    picked = pick(spectra, quality, sources)
    per_slot = sources.shape[0] // 4
    half = per_slot // 2
    receivers = whiten(spectra, quality)
    table = lag_table(spectra.shape[2], LAGS)
    gathered = [sum_over_chan(picked[t], picked[4 + t], chan_count) for t in range(4)]
    send = lambda value, pairs: lax.ppermute(value, "hour", pairs)
    mine = [
        [lags_of(*gathered[t], receivers, table, h * half, half) for h in range(2)] for t in range(4)
    ]
    inward = [[send(mine[t][h], INWARD) for h in range(2)] for t in range(3)]
    middle = [[send(add(mine[t][h], inward[t][h]), MIDDLE) for h in range(2)] for t in range(2)]
    outward = [send(add(mine[2][h], middle[0][h]), OUTWARD) for h in range(2)]
    return jnp.concatenate(
        [add(mine[3][h], inward[2][h], middle[1][h], outward[h]) for h in range(2)], 0
    )


def solution(mesh):
    placed = (P(None, "hour", None, "chan"), P("hour", "chan"), P())
    return jax.shard_map(
        functools.partial(body, mesh.shape["chan"]),
        mesh=mesh,
        in_specs=placed,
        out_specs=P("hour", None, "chan"),
        check_vma=False,
    )
```

```python
import functools
import math

import jax
import jax.numpy as jnp
from jax import lax
from jax.experimental import pallas as pl
from jax.experimental.pallas import tpu as pltpu
from jax.sharding import PartitionSpec as P

LAGS = 512
GROUP = 16
ORDER = ((3, 2, 1, 0), (3, 2, 0, 1), (0, 1, 3, 2), (0, 1, 2, 3))
SPLITS = (4, 4)
INWARD = ((0, 1), (3, 2))
MIDDLE = ((1, 2), (2, 1))
OUTWARD = ((1, 0), (2, 3))
MIB = 1024 * 1024
COST = pl.CostEstimate(flops=1, bytes_accessed=1, transcendentals=0)

HBM = pl.BlockSpec(memory_space=pltpu.HBM)
ANY = pl.BlockSpec(memory_space=pl.ANY)
VMEM = pl.BlockSpec(memory_space=pltpu.VMEM)


def quarter_of(hour, slot):
    quarter = jnp.int32(ORDER[0][slot])
    for row in range(1, 4):
        quarter = jnp.where(hour == row, jnp.int32(ORDER[row][slot]), quarter)
    return quarter


def shares(window_count, freq_count):
    middle = (freq_count // (2 * GROUP) + 1) // 2 * 2 * GROUP
    half = window_count // 2
    return [
        ((low, low + half), bins) for low in (0, half) for bins in ((0, middle), (middle, freq_count))
    ]


def front_kernel(
    sources_hbm, spectra_hbm, quality_hbm,
    own_first_ref, own_second_ref, own_rest_ref, other_first_ref, other_second_ref, other_rest_ref,
    scale_ref, data_ref,
    sources_ref, quality_ref, sems, small_sems,
):
    small = [
        pltpu.make_async_copy(sources_hbm, sources_ref, small_sems.at[0]),
        pltpu.make_async_copy(quality_hbm, quality_ref, small_sems.at[1]),
    ]
    _, window_count, freq_count, channels_here = data_ref.shape
    large = []
    for at, (windows, bins) in enumerate(shares(window_count, freq_count)):
        part = (slice(None), pl.ds(windows[0], windows[1] - windows[0]), pl.ds(bins[0], bins[1] - bins[0]))
        large.append(pltpu.make_async_copy(spectra_hbm.at[part], data_ref.at[part], sems.at[at]))
    for copy in small + large:
        copy.start()
    source_count = sources_ref.shape[0]
    per_slot = source_count // 4
    wide = window_count * GROUP
    chan = lax.axis_index("chan")
    hour = lax.axis_index("hour")
    even = (chan % 2) == 0
    for copy in small:
        copy.wait()
    row = lax.broadcasted_iota(jnp.int32, (source_count, channels_here), 0)
    lane = lax.broadcasted_iota(jnp.int32, (source_count, channels_here), 1)
    wanted = jnp.full((source_count, channels_here), -1, jnp.int32)
    for slot in range(4):
        first = quarter_of(hour, slot) * per_slot
        for at in range(per_slot):
            wanted = jnp.where(row == slot * per_slot + at, sources_ref[first + at], wanted)
    onehot = (wanted - chan * channels_here == lane).astype(jnp.float32).astype(jnp.bfloat16)
    quality = quality_ref[...].astype(jnp.float32)
    usable = lax.dot_general(
        onehot, quality.astype(jnp.bfloat16), (((1,), (1,)), ((), ())), preferred_element_type=jnp.float32
    )
    spread = (
        lax.broadcasted_iota(jnp.int32, (window_count, wide), 1) // GROUP
        == lax.broadcasted_iota(jnp.int32, (window_count, wide), 0)
    )
    usable = jnp.dot(
        usable.astype(jnp.bfloat16),
        spread.astype(jnp.float32).astype(jnp.bfloat16),
        preferred_element_type=jnp.float32,
    )
    narrow = wide // 2
    totals = {}
    for copy, (windows, bins) in zip(large, shares(window_count, freq_count)):
        copy.wait()
        lanes = slice(windows[0] * GROUP, windows[1] * GROUP)
        usable_here = jnp.concatenate([usable[:, lanes]] * 2, 1)
        total = totals.get(windows, jnp.zeros((windows[1] - windows[0], 8, channels_here), jnp.float32))
        for pair in range(bins[0] // (2 * GROUP), bins[1] // (2 * GROUP)):
            picked = []
            for part in range(2):
                both = []
                for group in (2 * pair, 2 * pair + 1):
                    columns = data_ref[
                        part, windows[0] : windows[1], group * GROUP : (group + 1) * GROUP, :
                    ]
                    value = columns.astype(jnp.float32)
                    square = value * value
                    total = total + (square[:, :8] + square[:, 8:])
                    both.append(columns.reshape(narrow, channels_here))
                picked.append(
                    lax.dot_general(
                        onehot,
                        jnp.concatenate(both, 0),
                        (((1,), (1,)), ((), ())),
                        preferred_element_type=jnp.float32,
                    )
                    * usable_here
                )
            own = jnp.where(even, picked[0], picked[1])
            other = jnp.where(even, picked[1], picked[0])
            for value, first_ref, second_ref, rest_ref in (
                (own, own_first_ref, own_second_ref, own_rest_ref),
                (other, other_first_ref, other_second_ref, other_rest_ref),
            ):
                for slot, ref in enumerate((first_ref, second_ref, rest_ref, rest_ref)):
                    rows = slice(slot * per_slot, (slot + 1) * per_slot)
                    at = pair * 16 + max(slot - 2, 0) * freq_count // GROUP * per_slot
                    both = jnp.concatenate([value[rows, :narrow], value[rows, narrow:]], 0)
                    ref[at : at + 16, lanes] = both.astype(jnp.bfloat16)
        totals[windows] = total
    power = jnp.concatenate([jnp.sum(total, axis=1) for total in totals.values()], 0) / freq_count
    scale_ref[...] = lax.rsqrt(power + 1e-06) * quality


def front(spectra, quality, sources):
    _, window_count, freq_count, channels_here = spectra.shape
    rows = freq_count // GROUP * sources.shape[0] // 4
    wide = window_count * GROUP
    steps = len(shares(window_count, freq_count))
    shape = lambda count: jax.ShapeDtypeStruct((count * rows, wide), jnp.bfloat16)
    return pl.pallas_call(
        front_kernel,
        in_specs=[HBM, HBM, HBM],
        out_specs=[VMEM] * 8,
        out_shape=[
            *(shape(slots) for slots in (1, 1, 2) * 2),
            jax.ShapeDtypeStruct(quality.shape, jnp.float32),
            jax.ShapeDtypeStruct(spectra.shape, jnp.bfloat16),
        ],
        scratch_shapes=[
            pltpu.SMEM(sources.shape, jnp.int32),
            pltpu.VMEM(quality.shape, jnp.int32),
            pltpu.SemaphoreType.DMA((steps,)),
            pltpu.SemaphoreType.DMA((2,)),
        ],
        compiler_params=pltpu.CompilerParams(vmem_limit_bytes=16 * MIB),
        cost_estimate=COST,
        name="pick_sources",
    )(*(pltpu.with_memory_space_constraint(value, pltpu.HBM) for value in (sources, spectra, quality)))


def whiten_kernel(data_ref, scale_ref, after_ref, out_ref):
    _, window_count, freq_count, _ = data_ref.shape
    step = freq_count // 5
    for window in range(window_count):
        scale = scale_ref[window : window + 1, :]

        def apply(i, carry):
            bins = pl.ds(pl.multiple_of(i * step, step), step)
            for part in range(2):
                value = data_ref[part, window, bins, :].astype(jnp.float32) * scale
                out_ref[part, window, bins, :] = value.astype(jnp.bfloat16)
            return carry

        lax.fori_loop(0, freq_count // step, apply, 0)


def whiten(data, scale, after):
    return pl.pallas_call(
        whiten_kernel,
        in_specs=[VMEM, VMEM, ANY],
        out_specs=VMEM,
        out_shape=jax.ShapeDtypeStruct(data.shape, jnp.bfloat16),
        compiler_params=pltpu.CompilerParams(vmem_limit_bytes=16 * MIB),
        cost_estimate=COST,
        name="whiten_receivers",
    )(data, scale, after)


def add_kernel(count, *refs):
    total = refs[0][...].astype(jnp.float32)
    for ref in refs[1:count]:
        total = total + ref[...].astype(jnp.float32)
    refs[-1][...] = total.astype(refs[-1].dtype)


def add_after(after, *values):
    return pl.pallas_call(
        functools.partial(add_kernel, len(values)),
        in_specs=[VMEM] * len(values) + [ANY],
        out_specs=VMEM,
        out_shape=jax.ShapeDtypeStruct(values[0].shape, values[0].dtype),
        compiler_params=pltpu.CompilerParams(vmem_limit_bytes=16 * MIB),
        cost_estimate=COST,
        name="add",
    )(*values, after)


def table_kernel(after_ref, out_ref):
    lag_count, columns = out_ref.shape
    freq_count = columns // 2
    highs = lag_count // GROUP

    def angle(count, lag_of, offset):
        lag = lag_of(lax.broadcasted_iota(jnp.int32, (count, columns), 0)).astype(jnp.float32)
        column = lax.broadcasted_iota(jnp.int32, (count, columns), 1).astype(jnp.float32)
        part = (column >= freq_count).astype(jnp.float32)
        turns = (column - part * freq_count + 1.0) * lag + part * offset
        turns = turns - columns * jnp.round(turns * (1.0 / columns))
        return turns * (math.pi / freq_count)

    high = angle(highs, lambda row: row * GROUP - lag_count // 2, freq_count // 2)
    low = angle(GROUP, lambda row: row, 0)
    cos_high, sin_high = jnp.cos(high), jnp.sin(high)
    cos_low, sin_low = jnp.cos(low) / freq_count, jnp.sin(low) / freq_count
    for row in range(highs):
        value = cos_high[row : row + 1] * cos_low - sin_high[row : row + 1] * sin_low
        out_ref[row * GROUP : (row + 1) * GROUP, :] = value.astype(jnp.bfloat16)


def lag_table(freq_count, lag_count, after):
    return pl.pallas_call(
        table_kernel,
        in_specs=[ANY],
        out_specs=VMEM,
        out_shape=jax.ShapeDtypeStruct((lag_count, 2 * freq_count), jnp.bfloat16),
        compiler_params=pltpu.CompilerParams(vmem_limit_bytes=16 * MIB),
        cost_estimate=COST,
        name="lag_table",
    )(after)


def lags_kernel(
    base, done,
    own_ref, other_ref, receivers_ref, table_ref, after_ref, out_ref, *refs,
):
    spec_ref, cross_ref = refs[-2:]
    count = 8
    _, window_count, freq_count, channels_here = receivers_ref.shape
    wide = own_ref.shape[1]
    groups = freq_count // GROUP
    even = (lax.axis_index("chan") % 2) == 0

    def load(i):
        rows = pl.ds(pl.multiple_of(base + i * 16, 16), 16)
        own = own_ref[rows, :].astype(jnp.float32)
        other = other_ref[rows, :].astype(jnp.float32)
        return jnp.where(even, own, other), jnp.where(even, other, own)

    def add(i, total):
        real, imag = load(i)
        square = real * real + imag * imag
        return total + square[:8] + square[8:]

    total = lax.fori_loop(0, groups // 2, add, jnp.zeros((8, wide), jnp.float32), unroll=5)
    same = (
        lax.broadcasted_iota(jnp.int32, (wide, wide), 0) // GROUP
        == lax.broadcasted_iota(jnp.int32, (wide, wide), 1) // GROUP
    ).astype(jnp.float32)
    power = jnp.dot(total, same, preferred_element_type=jnp.float32, precision=lax.Precision.HIGHEST)
    scale = lax.rsqrt(power / freq_count + 1e-06)
    scale = jnp.concatenate([scale, scale], 0)

    def apply(i, carry):
        rows = pl.ds(pl.multiple_of(i * 16, 16), 16)
        for part, value in enumerate(load(i)):
            spec_ref[part, rows, :] = (value * scale).astype(jnp.bfloat16).astype(jnp.float32)
        return carry

    lax.fori_loop(0, groups // 2, apply, 0, unroll=5)

    diagonal = [
        lax.broadcasted_iota(jnp.int32, (8, wide), 1) % GROUP
        == lax.broadcasted_iota(jnp.int32, (8, wide), 0) + low
        for low in (0, 8)
    ]
    zero = jnp.zeros((8, wide), jnp.float32)

    def cross_of(group, carry):
        tiles = []
        for part in range(2):
            rows = spec_ref[part, pl.ds(pl.multiple_of(group * 8, 8), 8), :]
            for at in range(count):
                row = jnp.broadcast_to(rows[at : at + 1, :], (8, wide))
                tiles += [jnp.where(mask, row, zero) for mask in diagonal]
        bins = pl.ds(pl.multiple_of(group * GROUP, GROUP), GROUP)
        real = receivers_ref[0, :, bins, :].reshape(wide, channels_here)
        imag = receivers_ref[1, :, bins, :].reshape(wide, channels_here)
        cross = jnp.dot(
            jnp.concatenate(tiles, 0).astype(jnp.bfloat16),
            jnp.concatenate([real, imag], 1),
            preferred_element_type=jnp.float32,
        )
        half = count * GROUP
        parts = (
            cross[:half, :channels_here] + cross[half:, channels_here:],
            cross[:half, channels_here:] - cross[half:, :channels_here],
        )
        for part, value in enumerate(parts):
            value = value.astype(jnp.bfloat16)
            rows = pl.ds(pl.multiple_of(part * freq_count + group * GROUP, GROUP), GROUP)
            for at in range(count):
                ref, pair = (cross_ref, at // 2) if at < done else (refs[0], (at - done) // 2)
                lanes = slice((at % 2) * channels_here, (at % 2 + 1) * channels_here)
                ref[pair, rows, lanes] = value[at * GROUP : (at + 1) * GROUP]
        return carry

    lax.fori_loop(0, groups, cross_of, 0, unroll=25)
    transform(cross_ref, table_ref, out_ref)


def transform(cross_ref, table_ref, out_ref):
    channels_here = out_ref.shape[2]
    rows = 128
    for pair in range(cross_ref.shape[0]):
        for block in range(table_ref.shape[0] // rows):
            lags = slice(block * rows, (block + 1) * rows)
            value = jnp.dot(
                table_ref[lags, :], cross_ref[pair], preferred_element_type=jnp.float32
            ).astype(jnp.bfloat16)
            out_ref[2 * pair, lags, :] = value[:, :channels_here]
            out_ref[2 * pair + 1, lags, :] = value[:, channels_here:]


def lags_of(own, other, receivers, table, base, done, after):
    _, window_count, freq_count, channels_here = receivers.shape
    wide = own.shape[1]
    count = 8
    cross = lambda sources: (sources // 2, 2 * freq_count, 2 * channels_here)
    out_shape = [jax.ShapeDtypeStruct((done, table.shape[0], channels_here), jnp.bfloat16)]
    if done < count:
        out_shape.append(jax.ShapeDtypeStruct(cross(count - done), jnp.bfloat16))
    return pl.pallas_call(
        functools.partial(lags_kernel, base, done),
        in_specs=[VMEM] * 4 + [ANY],
        out_specs=[VMEM] * len(out_shape),
        out_shape=out_shape,
        scratch_shapes=[
            pltpu.VMEM((2, freq_count // GROUP * 8, wide), jnp.float32),
            pltpu.VMEM(cross(done), jnp.bfloat16),
        ],
        compiler_params=pltpu.CompilerParams(vmem_limit_bytes=16 * MIB),
        cost_estimate=COST,
        name="lags",
    )(own, other, receivers, table, after)


def lags_of_rest(cross, table, after):
    pairs, _, lanes = cross.shape
    return pl.pallas_call(
        lambda cross_ref, table_ref, after_ref, out_ref: transform(cross_ref, table_ref, out_ref),
        in_specs=[VMEM, VMEM, ANY],
        out_specs=VMEM,
        out_shape=jax.ShapeDtypeStruct((2 * pairs, table.shape[0], lanes // 2), jnp.bfloat16),
        compiler_params=pltpu.CompilerParams(vmem_limit_bytes=16 * MIB),
        cost_estimate=COST,
        name="lags_rest",
    )(cross, table, after)


def chip_stages(chan_count):
    bits = [1 << b for b in range(1, chan_count.bit_length() - 1)]
    turned = bits[1:] + bits[:1]
    return [
        [(i, i ^ (odd_bit if i % 2 else even_bit)) for i in range(chan_count)]
        for even_bit, odd_bit in zip(bits, turned)
    ]


def body(chan_count, spectra, quality, sources):
    own, other, (scale, data) = (lambda v: (v[:3], v[3:6], v[6:]))(front(spectra, quality, sources))
    freq_count = spectra.shape[2]
    slot_rows = own[0].shape[0]
    stages = chip_stages(chan_count)
    cores = [(i, i ^ 1) for i in range(chan_count)]
    over_chan = lambda value, pairs: lax.ppermute(value, "chan", pairs)
    over_hour = lambda value, pairs: lax.ppermute(value, "hour", pairs)

    moved = [over_chan(value, cores) for value in other]
    state = list(own)

    def receive(at, pairs):
        state[at] = add_after(last, state[at], moved[at])
        moved[at] = over_chan(state[at], pairs)
        return state[at]

    last = scale
    last = receive(0, stages[0])
    table = last = lag_table(freq_count, LAGS, last)
    for pairs in stages[1:]:
        last = receive(0, pairs)
    last = receive(1, stages[0])
    receivers = last = whiten(data, scale, last)
    last = receive(0, cores)
    for pairs in stages[1:]:
        last = receive(1, pairs)
    last = receive(2, stages[0])

    def lags(chunk, base=0, done=8):
        return lags_of(*chunk, receivers, table, base, done, last)

    mine = [[], [], [], []]
    inward = [[], [], []]
    middle = [[], []]

    def send_inward(slot, value):
        mine[slot].append(value)
        inward[slot].append(over_hour(value, INWARD))
        return value

    def send_middle(slot, at):
        value = add_after(last, mine[slot][at], inward[slot][at])
        middle[slot].append(over_hour(value, MIDDLE))
        return value

    value, cross = lags((state[0], moved[0]), 0, SPLITS[0])
    last = send_inward(0, value)
    last = receive(1, cores)
    for pairs in stages[1:]:
        last = receive(2, pairs)
    last = send_inward(0, lags_of_rest(cross, table, last))
    last = receive(2, cores)
    value, cross = lags((state[1], moved[1]), 0, SPLITS[1])
    last = send_inward(1, value)
    last = send_inward(1, lags_of_rest(cross, table, last))
    last = send_middle(0, 0)
    last = send_middle(0, 1)
    rest = (state[2], moved[2])
    last = send_inward(2, lags(rest)[0])
    last = own_lags = lags(rest, slot_rows)[0]
    outward = []
    cuts = (0, SPLITS[0], 8)
    sums = [mine[2][0][low:high] for low, high in zip(cuts, cuts[1:])]
    last = send_middle(1, 0)
    for at in range(2):
        last = add_after(last, sums[at], middle[0][at])
        outward.append(over_hour(last, OUTWARD))
    last = send_middle(1, 1)
    whole = lambda values: values[0] if len(values) == 1 else jnp.concatenate(values, 0)
    values = [own_lags] + [whole(values) for values in (middle[1], outward, inward[2])]
    return sum(value.astype(jnp.float32) for value in values).astype(jnp.bfloat16)


def solution(mesh):
    placed = (P(None, "hour", None, "chan"), P("hour", "chan"), P())
    return jax.shard_map(
        functools.partial(body, mesh.shape["chan"]),
        mesh=mesh,
        in_specs=placed,
        out_specs=P("hour", None, "chan"),
        check_vma=False,
    )
```

```python
import functools
import math

import jax
import jax.numpy as jnp
from jax import lax
from jax.experimental import pallas as pl
from jax.experimental.pallas import tpu as pltpu
from jax.sharding import PartitionSpec as P

LAGS = 512
GROUP = 16
ORDER = ((3, 2, 1, 0), (3, 2, 0, 1), (0, 1, 3, 2), (0, 1, 2, 3))
SPLITS = (4, 2, 8, 8)
STEPS = "r0 r1 t r0 w r1 r2 r0 l0 r1 k0 r2 l1 m0 r2 k1 l3 n0 l2 m1 f g h n1 p".split()
INWARD = ((0, 1), (3, 2))
MIDDLE = ((1, 2), (2, 1))
OUTWARD = ((1, 0), (2, 3))
MIB = 1024 * 1024
COST = pl.CostEstimate(flops=1, bytes_accessed=1, transcendentals=0)

HBM = pl.BlockSpec(memory_space=pltpu.HBM)
ANY = pl.BlockSpec(memory_space=pl.ANY)
VMEM = pl.BlockSpec(memory_space=pltpu.VMEM)


def quarter_of(hour, slot):
    quarter = jnp.int32(ORDER[0][slot])
    for row in range(1, 4):
        quarter = jnp.where(hour == row, jnp.int32(ORDER[row][slot]), quarter)
    return quarter


def shares(window_count, freq_count):
    middle = (freq_count // (2 * GROUP) + 1) // 2 * 2 * GROUP
    half = window_count // 2
    return [
        ((low, low + half), bins) for low in (0, half) for bins in ((0, middle), (middle, freq_count))
    ]


def front_kernel(
    sources_hbm, spectra_hbm, quality_hbm,
    own_first_ref, own_second_ref, own_rest_ref, other_first_ref, other_second_ref, other_rest_ref,
    scale_ref, data_ref,
    sources_ref, quality_ref, sems, small_sems,
):
    small = [
        pltpu.make_async_copy(sources_hbm, sources_ref, small_sems.at[0]),
        pltpu.make_async_copy(quality_hbm, quality_ref, small_sems.at[1]),
    ]
    _, window_count, freq_count, channels_here = data_ref.shape
    large = []
    for at, (windows, bins) in enumerate(shares(window_count, freq_count)):
        part = (slice(None), pl.ds(windows[0], windows[1] - windows[0]), pl.ds(bins[0], bins[1] - bins[0]))
        large.append(pltpu.make_async_copy(spectra_hbm.at[part], data_ref.at[part], sems.at[at]))
    for copy in small + large:
        copy.start()
    source_count = sources_ref.shape[0]
    per_slot = source_count // 4
    wide = window_count * GROUP
    chan = lax.axis_index("chan")
    hour = lax.axis_index("hour")
    even = (chan % 2) == 0
    for copy in small:
        copy.wait()
    row = lax.broadcasted_iota(jnp.int32, (source_count, channels_here), 0)
    lane = lax.broadcasted_iota(jnp.int32, (source_count, channels_here), 1)
    wanted = jnp.full((source_count, channels_here), -1, jnp.int32)
    for slot in range(4):
        first = quarter_of(hour, slot) * per_slot
        for at in range(per_slot):
            wanted = jnp.where(row == slot * per_slot + at, sources_ref[first + at], wanted)
    onehot = (wanted - chan * channels_here == lane).astype(jnp.float32).astype(jnp.bfloat16)
    quality = quality_ref[...].astype(jnp.float32)
    usable = lax.dot_general(
        onehot, quality.astype(jnp.bfloat16), (((1,), (1,)), ((), ())), preferred_element_type=jnp.float32
    )
    spread = (
        lax.broadcasted_iota(jnp.int32, (window_count, wide), 1) // GROUP
        == lax.broadcasted_iota(jnp.int32, (window_count, wide), 0)
    )
    usable = jnp.dot(
        usable.astype(jnp.bfloat16),
        spread.astype(jnp.float32).astype(jnp.bfloat16),
        preferred_element_type=jnp.float32,
    )
    narrow = wide // 2
    totals = {}
    for copy, (windows, bins) in zip(large, shares(window_count, freq_count)):
        copy.wait()
        lanes = slice(windows[0] * GROUP, windows[1] * GROUP)
        usable_here = jnp.concatenate([usable[:, lanes]] * 2, 1)
        total = totals.get(windows, jnp.zeros((windows[1] - windows[0], 8, channels_here), jnp.float32))
        for pair in range(bins[0] // (2 * GROUP), bins[1] // (2 * GROUP)):
            picked = []
            for part in range(2):
                both = []
                for group in (2 * pair, 2 * pair + 1):
                    columns = data_ref[
                        part, windows[0] : windows[1], group * GROUP : (group + 1) * GROUP, :
                    ]
                    value = columns.astype(jnp.float32)
                    square = value * value
                    total = total + (square[:, :8] + square[:, 8:])
                    both.append(columns.reshape(narrow, channels_here))
                picked.append(
                    lax.dot_general(
                        onehot,
                        jnp.concatenate(both, 0),
                        (((1,), (1,)), ((), ())),
                        preferred_element_type=jnp.float32,
                    )
                    * usable_here
                )
            own = jnp.where(even, picked[0], picked[1])
            other = jnp.where(even, picked[1], picked[0])
            for value, first_ref, second_ref, rest_ref in (
                (own, own_first_ref, own_second_ref, own_rest_ref),
                (other, other_first_ref, other_second_ref, other_rest_ref),
            ):
                for slot, ref in enumerate((first_ref, second_ref, rest_ref, rest_ref)):
                    rows = slice(slot * per_slot, (slot + 1) * per_slot)
                    at = pair * 16 + max(slot - 2, 0) * freq_count // GROUP * per_slot
                    both = jnp.concatenate([value[rows, :narrow], value[rows, narrow:]], 0)
                    ref[at : at + 16, lanes] = both.astype(jnp.bfloat16)
        totals[windows] = total
    power = jnp.concatenate([jnp.sum(total, axis=1) for total in totals.values()], 0) / freq_count
    scale_ref[...] = lax.rsqrt(power + 1e-06) * quality


def front(spectra, quality, sources):
    _, window_count, freq_count, channels_here = spectra.shape
    rows = freq_count // GROUP * sources.shape[0] // 4
    wide = window_count * GROUP
    steps = len(shares(window_count, freq_count))
    shape = lambda count: jax.ShapeDtypeStruct((count * rows, wide), jnp.bfloat16)
    return pl.pallas_call(
        front_kernel,
        in_specs=[HBM, HBM, HBM],
        out_specs=[VMEM] * 8,
        out_shape=[
            *(shape(slots) for slots in (1, 1, 2) * 2),
            jax.ShapeDtypeStruct(quality.shape, jnp.float32),
            jax.ShapeDtypeStruct(spectra.shape, jnp.bfloat16),
        ],
        scratch_shapes=[
            pltpu.SMEM(sources.shape, jnp.int32),
            pltpu.VMEM(quality.shape, jnp.int32),
            pltpu.SemaphoreType.DMA((steps,)),
            pltpu.SemaphoreType.DMA((2,)),
        ],
        compiler_params=pltpu.CompilerParams(vmem_limit_bytes=16 * MIB),
        cost_estimate=COST,
        name="pick_sources",
    )(*(pltpu.with_memory_space_constraint(value, pltpu.HBM) for value in (sources, spectra, quality)))


def whiten_kernel(data_ref, scale_ref, after_ref, out_ref):
    _, window_count, freq_count, _ = data_ref.shape
    step = freq_count // 5
    for window in range(window_count):
        scale = scale_ref[window : window + 1, :]

        def apply(i, carry):
            bins = pl.ds(pl.multiple_of(i * step, step), step)
            for part in range(2):
                value = data_ref[part, window, bins, :].astype(jnp.float32) * scale
                out_ref[part, window, bins, :] = value.astype(jnp.bfloat16)
            return carry

        lax.fori_loop(0, freq_count // step, apply, 0)


def whiten(data, scale, after):
    return pl.pallas_call(
        whiten_kernel,
        in_specs=[VMEM, VMEM, ANY],
        out_specs=VMEM,
        out_shape=jax.ShapeDtypeStruct(data.shape, jnp.bfloat16),
        compiler_params=pltpu.CompilerParams(vmem_limit_bytes=16 * MIB),
        cost_estimate=COST,
        name="whiten_receivers",
    )(data, scale, after)


def add_kernel(count, *refs):
    total = refs[0][...].astype(jnp.float32)
    for ref in refs[1:count]:
        total = total + ref[...].astype(jnp.float32)
    refs[-1][...] = total.astype(refs[-1].dtype)


def add_after(after, *values):
    return pl.pallas_call(
        functools.partial(add_kernel, len(values)),
        in_specs=[VMEM] * len(values) + [ANY],
        out_specs=VMEM,
        out_shape=jax.ShapeDtypeStruct(values[0].shape, values[0].dtype),
        compiler_params=pltpu.CompilerParams(vmem_limit_bytes=16 * MIB),
        cost_estimate=COST,
        name="add",
    )(*values, after)


def table_kernel(after_ref, out_ref):
    lag_count, columns = out_ref.shape
    freq_count = columns // 2
    highs = lag_count // GROUP

    def angle(count, lag_of, offset):
        lag = lag_of(lax.broadcasted_iota(jnp.int32, (count, columns), 0)).astype(jnp.float32)
        column = lax.broadcasted_iota(jnp.int32, (count, columns), 1).astype(jnp.float32)
        part = (column >= freq_count).astype(jnp.float32)
        turns = (column - part * freq_count + 1.0) * lag + part * offset
        turns = turns - columns * jnp.round(turns * (1.0 / columns))
        return turns * (math.pi / freq_count)

    high = angle(highs, lambda row: row * GROUP - lag_count // 2, freq_count // 2)
    low = angle(GROUP, lambda row: row, 0)
    cos_high, sin_high = jnp.cos(high), jnp.sin(high)
    cos_low, sin_low = jnp.cos(low) / freq_count, jnp.sin(low) / freq_count
    for row in range(highs):
        value = cos_high[row : row + 1] * cos_low - sin_high[row : row + 1] * sin_low
        out_ref[row * GROUP : (row + 1) * GROUP, :] = value.astype(jnp.bfloat16)


def lag_table(freq_count, lag_count, after):
    return pl.pallas_call(
        table_kernel,
        in_specs=[ANY],
        out_specs=VMEM,
        out_shape=jax.ShapeDtypeStruct((lag_count, 2 * freq_count), jnp.bfloat16),
        compiler_params=pltpu.CompilerParams(vmem_limit_bytes=16 * MIB),
        cost_estimate=COST,
        name="lag_table",
    )(after)


def lags_kernel(
    base, done,
    own_ref, other_ref, receivers_ref, table_ref, after_ref, out_ref, *refs,
):
    spec_ref, cross_ref = refs[-2:]
    count = 8
    _, window_count, freq_count, channels_here = receivers_ref.shape
    wide = own_ref.shape[1]
    groups = freq_count // GROUP
    even = (lax.axis_index("chan") % 2) == 0

    def load(i):
        rows = pl.ds(pl.multiple_of(base + i * 16, 16), 16)
        own = own_ref[rows, :].astype(jnp.float32)
        other = other_ref[rows, :].astype(jnp.float32)
        return jnp.where(even, own, other), jnp.where(even, other, own)

    def add(i, total):
        real, imag = load(i)
        square = real * real + imag * imag
        return total + square[:8] + square[8:]

    total = lax.fori_loop(0, groups // 2, add, jnp.zeros((8, wide), jnp.float32), unroll=5)
    same = (
        lax.broadcasted_iota(jnp.int32, (wide, wide), 0) // GROUP
        == lax.broadcasted_iota(jnp.int32, (wide, wide), 1) // GROUP
    ).astype(jnp.float32)
    power = jnp.dot(total, same, preferred_element_type=jnp.float32, precision=lax.Precision.HIGHEST)
    scale = lax.rsqrt(power / freq_count + 1e-06)
    scale = jnp.concatenate([scale, scale], 0)

    def apply(i, carry):
        rows = pl.ds(pl.multiple_of(i * 16, 16), 16)
        for part, value in enumerate(load(i)):
            spec_ref[part, rows, :] = (value * scale).astype(jnp.bfloat16).astype(jnp.float32)
        return carry

    lax.fori_loop(0, groups // 2, apply, 0, unroll=5)

    diagonal = [
        lax.broadcasted_iota(jnp.int32, (8, wide), 1) % GROUP
        == lax.broadcasted_iota(jnp.int32, (8, wide), 0) + low
        for low in (0, 8)
    ]
    zero = jnp.zeros((8, wide), jnp.float32)

    def cross_of(group, carry):
        tiles = []
        for part in range(2):
            rows = spec_ref[part, pl.ds(pl.multiple_of(group * 8, 8), 8), :]
            for at in range(count):
                row = jnp.broadcast_to(rows[at : at + 1, :], (8, wide))
                tiles += [jnp.where(mask, row, zero) for mask in diagonal]
        bins = pl.ds(pl.multiple_of(group * GROUP, GROUP), GROUP)
        real = receivers_ref[0, :, bins, :].reshape(wide, channels_here)
        imag = receivers_ref[1, :, bins, :].reshape(wide, channels_here)
        cross = jnp.dot(
            jnp.concatenate(tiles, 0).astype(jnp.bfloat16),
            jnp.concatenate([real, imag], 1),
            preferred_element_type=jnp.float32,
        )
        half = count * GROUP
        parts = (
            cross[:half, :channels_here] + cross[half:, channels_here:],
            cross[:half, channels_here:] - cross[half:, :channels_here],
        )
        for part, value in enumerate(parts):
            value = value.astype(jnp.bfloat16)
            rows = pl.ds(pl.multiple_of(part * freq_count + group * GROUP, GROUP), GROUP)
            for at in range(count):
                ref, pair = (cross_ref, at // 2) if at < done else (refs[0], (at - done) // 2)
                lanes = slice((at % 2) * channels_here, (at % 2 + 1) * channels_here)
                ref[pair, rows, lanes] = value[at * GROUP : (at + 1) * GROUP]
        return carry

    lax.fori_loop(0, groups, cross_of, 0, unroll=25)
    transform(cross_ref, table_ref, out_ref)


def transform(cross_ref, table_ref, out_ref):
    channels_here = out_ref.shape[2]
    rows = 128
    for pair in range(cross_ref.shape[0]):
        for block in range(table_ref.shape[0] // rows):
            lags = slice(block * rows, (block + 1) * rows)
            value = jnp.dot(
                table_ref[lags, :], cross_ref[pair], preferred_element_type=jnp.float32
            ).astype(jnp.bfloat16)
            out_ref[2 * pair, lags, :] = value[:, :channels_here]
            out_ref[2 * pair + 1, lags, :] = value[:, channels_here:]


def lags_of(own, other, receivers, table, base, done, after):
    _, window_count, freq_count, channels_here = receivers.shape
    wide = own.shape[1]
    count = 8
    cross = lambda sources: (sources // 2, 2 * freq_count, 2 * channels_here)
    out_shape = [jax.ShapeDtypeStruct((done, table.shape[0], channels_here), jnp.bfloat16)]
    if done < count:
        out_shape.append(jax.ShapeDtypeStruct(cross(count - done), jnp.bfloat16))
    return pl.pallas_call(
        functools.partial(lags_kernel, base, done),
        in_specs=[VMEM] * 4 + [ANY],
        out_specs=[VMEM] * len(out_shape),
        out_shape=out_shape,
        scratch_shapes=[
            pltpu.VMEM((2, freq_count // GROUP * 8, wide), jnp.float32),
            pltpu.VMEM(cross(done), jnp.bfloat16),
        ],
        compiler_params=pltpu.CompilerParams(vmem_limit_bytes=16 * MIB),
        cost_estimate=COST,
        name="lags",
    )(own, other, receivers, table, after)


def lags_of_rest(cross, table, after):
    pairs, _, lanes = cross.shape
    return pl.pallas_call(
        lambda cross_ref, table_ref, after_ref, out_ref: transform(cross_ref, table_ref, out_ref),
        in_specs=[VMEM, VMEM, ANY],
        out_specs=VMEM,
        out_shape=jax.ShapeDtypeStruct((2 * pairs, table.shape[0], lanes // 2), jnp.bfloat16),
        compiler_params=pltpu.CompilerParams(vmem_limit_bytes=16 * MIB),
        cost_estimate=COST,
        name="lags_rest",
    )(cross, table, after)


def sum_kernel(firsts, low, *refs):
    out_ref, rest = refs[len(firsts) + 1], refs[len(firsts) + 2 :]
    total_ref = rest[0] if rest else out_ref
    copies = []
    for source in range(low, low + out_ref.shape[0]):
        total = 0.0
        for first, ref in zip(firsts, refs):
            if first <= source < first + ref.shape[0]:
                total = total + ref[source - first].astype(jnp.float32)
        total_ref[source - low] = total.astype(total_ref.dtype)
        if rest:
            copies.append(
                pltpu.make_async_copy(total_ref.at[source], out_ref.at[source], rest[1].at[source])
            )
            copies[-1].start()
    for copy in copies:
        copy.wait()


def sum_of(parts, low, high, dtype, after, final=False):
    firsts, values = zip(*parts)
    shape = (high - low,) + values[0].shape[1:]
    scratch = [pltpu.VMEM(shape, dtype), pltpu.SemaphoreType.DMA((high - low,))]
    return pl.pallas_call(
        functools.partial(sum_kernel, firsts, low),
        in_specs=[VMEM] * len(values) + [ANY],
        out_specs=HBM if final else VMEM,
        out_shape=jax.ShapeDtypeStruct(shape, dtype),
        scratch_shapes=scratch if final else [],
        compiler_params=pltpu.CompilerParams(vmem_limit_bytes=16 * MIB),
        cost_estimate=COST,
        name="sum",
    )(*values, after)


def chip_stages(chan_count):
    bits = [1 << b for b in range(1, chan_count.bit_length() - 1)]
    turned = bits[1:] + bits[:1]
    return [
        [(i, i ^ (odd_bit if i % 2 else even_bit)) for i in range(chan_count)]
        for even_bit, odd_bit in zip(bits, turned)
    ]


def body(chan_count, spectra, quality, sources):
    freq_count = spectra.shape[2]
    stages = chip_stages(chan_count)
    cores = [(i, i ^ 1) for i in range(chan_count)]
    over_chan = lambda value, pairs: lax.ppermute(value, "chan", pairs)
    over_hour = lambda value, pairs: lax.ppermute(value, "hour", pairs)

    front_out = front(spectra, quality, sources)
    (*state, scale, data) = front_out[:3] + front_out[6:]
    slot_rows = state[0].shape[0]
    moved = [over_chan(value, cores) for value in front_out[3:6]]
    passes = [0, 0, 0]
    made, mine, cross, middle, outward = {}, {}, {}, {}, {}
    inward = {}
    cuts = (0, SPLITS[0], 8)
    last = scale
    for step in STEPS:
        kind, at = step[0], int(step[1:] or 0)
        if kind == "r":
            for pairs in (stages[:1], stages[1:], [cores])[passes[at]]:
                last = state[at] = add_after(last, state[at], moved[at])
                moved[at] = over_chan(last, pairs)
            passes[at] += 1
        elif kind == "t":
            table = last = lag_table(freq_count, LAGS, last)
        elif kind == "w":
            receivers = last = whiten(data, scale, last)
        elif kind in "lk":
            if kind == "l":
                chunk = min(at, 2)
                values = lags_of(
                    state[chunk], moved[chunk], receivers, table, slot_rows * (at - chunk), SPLITS[at], last
                )
                last = values[0]
                cross[at] = values[-1]
            else:
                last = lags_of_rest(cross[at], table, last)
            mine[at, kind] = last
            if at < 3:
                inward[at, kind] = over_hour(last, INWARD)
        elif kind in "mn":
            which = "l" if kind == "m" else "k"
            last = add_after(last, mine[at, which], inward[at, which])
            middle[at, which] = over_hour(last, MIDDLE)
        elif kind in "fg":
            which, part = ("l", 0) if kind == "f" else ("k", 1)
            parts = [(0, mine[2, "l"]), (cuts[part], middle[0, which])]
            last = sum_of(parts, cuts[part], cuts[part + 1], jnp.bfloat16, last)
            outward[which] = over_hour(last, OUTWARD)
        elif kind == "h":
            parts = [(0, mine[3, "l"]), (0, outward["l"]), (0, middle[1, "l"])]
            early = last = sum_of(parts, 0, cuts[1], jnp.float32, last)
        elif kind == "p":
            parts = [(0, early), (cuts[1], mine[3, "l"][cuts[1] :]), (cuts[1], outward["k"])]
            parts += [(SPLITS[1], middle[1, "k"])]
            last = sum_of(parts, 0, 8, jnp.float32, last)
    return sum_of([(0, last), (0, inward[2, "l"])], 0, 8, jnp.bfloat16, last, final=True)


def solution(mesh):
    placed = (P(None, "hour", None, "chan"), P("hour", "chan"), P())
    return jax.shard_map(
        functools.partial(body, mesh.shape["chan"]),
        mesh=mesh,
        in_specs=placed,
        out_specs=P("hour", None, "chan"),
        check_vma=False,
    )
```

```python
import functools
import math

import jax
import jax.numpy as jnp
from jax import lax
from jax.experimental import pallas as pl
from jax.experimental.pallas import tpu as pltpu
from jax.sharding import PartitionSpec as P

LAGS = 512
GROUP = 16
ORDER = ((3, 2, 1, 0), (3, 2, 0, 1), (0, 1, 3, 2), (0, 1, 2, 3))
SPLITS = (4, 2, 8, 8)
STEPS = (
    "r0", "r1", "t", "r0", "w", "r1", "r2", "r0", "l0", "i0", "r1", "k0",
    "r2", "l1", "m0", "r2", "k1", "n0", "l2", "m1", "f", "l3", "g", "h", "n1", "p",
)
INWARD = ((0, 1), (3, 2))
MIDDLE = ((1, 2), (2, 1))
OUTWARD = ((1, 0), (2, 3))
ENDS, INNER = (0, 3), (1, 2)
MIB = 1024 * 1024
COST = pl.CostEstimate(flops=1, bytes_accessed=1, transcendentals=0)

HBM = pl.BlockSpec(memory_space=pltpu.HBM)
ANY = pl.BlockSpec(memory_space=pl.ANY)
VMEM = pl.BlockSpec(memory_space=pltpu.VMEM)


def quarter_of(hour, slot):
    quarter = jnp.int32(ORDER[0][slot])
    for row in range(1, 4):
        quarter = jnp.where(hour == row, jnp.int32(ORDER[row][slot]), quarter)
    return quarter


def shares(window_count, freq_count):
    middle = (freq_count // (2 * GROUP) + 1) // 2 * 2 * GROUP
    half = window_count // 2
    return [
        ((low, low + half), bins) for low in (0, half) for bins in ((0, middle), (middle, freq_count))
    ]


def front_kernel(
    sources_hbm, spectra_hbm, quality_hbm,
    own_first_ref, own_second_ref, own_rest_ref, other_first_ref, other_second_ref, other_rest_ref,
    scale_ref, data_ref,
    sources_ref, quality_ref, sems, small_sems,
):
    small = [
        pltpu.make_async_copy(sources_hbm, sources_ref, small_sems.at[0]),
        pltpu.make_async_copy(quality_hbm, quality_ref, small_sems.at[1]),
    ]
    _, window_count, freq_count, channels_here = data_ref.shape
    large = []
    for at, (windows, bins) in enumerate(shares(window_count, freq_count)):
        part = (slice(None), pl.ds(windows[0], windows[1] - windows[0]), pl.ds(bins[0], bins[1] - bins[0]))
        large.append(pltpu.make_async_copy(spectra_hbm.at[part], data_ref.at[part], sems.at[at]))
    for copy in small + large:
        copy.start()
    source_count = sources_ref.shape[0]
    per_slot = source_count // 4
    wide = window_count * GROUP
    chan = lax.axis_index("chan")
    hour = lax.axis_index("hour")
    even = (chan % 2) == 0
    for copy in small:
        copy.wait()
    row = lax.broadcasted_iota(jnp.int32, (source_count, channels_here), 0)
    lane = lax.broadcasted_iota(jnp.int32, (source_count, channels_here), 1)
    wanted = jnp.full((source_count, channels_here), -1, jnp.int32)
    for slot in range(4):
        first = quarter_of(hour, slot) * per_slot
        for at in range(per_slot):
            wanted = jnp.where(row == slot * per_slot + at, sources_ref[first + at], wanted)
    onehot = (wanted - chan * channels_here == lane).astype(jnp.float32).astype(jnp.bfloat16)
    quality = quality_ref[...].astype(jnp.float32)
    usable = lax.dot_general(
        onehot, quality.astype(jnp.bfloat16), (((1,), (1,)), ((), ())), preferred_element_type=jnp.float32
    )
    spread = (
        lax.broadcasted_iota(jnp.int32, (window_count, wide), 1) // GROUP
        == lax.broadcasted_iota(jnp.int32, (window_count, wide), 0)
    )
    usable = jnp.dot(
        usable.astype(jnp.bfloat16),
        spread.astype(jnp.float32).astype(jnp.bfloat16),
        preferred_element_type=jnp.float32,
    )
    narrow = wide // 2
    totals = {}
    for copy, (windows, bins) in zip(large, shares(window_count, freq_count)):
        copy.wait()
        lanes = slice(windows[0] * GROUP, windows[1] * GROUP)
        usable_here = jnp.concatenate([usable[:, lanes]] * 2, 1)
        total = totals.get(windows, jnp.zeros((windows[1] - windows[0], 8, channels_here), jnp.float32))
        for pair in range(bins[0] // (2 * GROUP), bins[1] // (2 * GROUP)):
            picked = []
            for part in range(2):
                both = []
                for group in (2 * pair, 2 * pair + 1):
                    columns = data_ref[
                        part, windows[0] : windows[1], group * GROUP : (group + 1) * GROUP, :
                    ]
                    value = columns.astype(jnp.float32)
                    square = value * value
                    total = total + (square[:, :8] + square[:, 8:])
                    both.append(columns.reshape(narrow, channels_here))
                picked.append(
                    lax.dot_general(
                        onehot,
                        jnp.concatenate(both, 0),
                        (((1,), (1,)), ((), ())),
                        preferred_element_type=jnp.float32,
                    )
                    * usable_here
                )
            own = jnp.where(even, picked[0], picked[1])
            other = jnp.where(even, picked[1], picked[0])
            for value, first_ref, second_ref, rest_ref in (
                (own, own_first_ref, own_second_ref, own_rest_ref),
                (other, other_first_ref, other_second_ref, other_rest_ref),
            ):
                for slot, ref in enumerate((first_ref, second_ref, rest_ref, rest_ref)):
                    rows = slice(slot * per_slot, (slot + 1) * per_slot)
                    at = pair * 16 + max(slot - 2, 0) * freq_count // GROUP * per_slot
                    both = jnp.concatenate([value[rows, :narrow], value[rows, narrow:]], 0)
                    ref[at : at + 16, lanes] = both.astype(jnp.bfloat16)
        totals[windows] = total
    power = jnp.concatenate([jnp.sum(total, axis=1) for total in totals.values()], 0) / freq_count
    scale_ref[...] = lax.rsqrt(power + 1e-06) * quality


def front(spectra, quality, sources):
    _, window_count, freq_count, channels_here = spectra.shape
    rows = freq_count // GROUP * sources.shape[0] // 4
    wide = window_count * GROUP
    steps = len(shares(window_count, freq_count))
    shape = lambda count: jax.ShapeDtypeStruct((count * rows, wide), jnp.bfloat16)
    return pl.pallas_call(
        front_kernel,
        in_specs=[HBM, HBM, HBM],
        out_specs=[VMEM] * 8,
        out_shape=[
            *(shape(slots) for slots in (1, 1, 2) * 2),
            jax.ShapeDtypeStruct(quality.shape, jnp.float32),
            jax.ShapeDtypeStruct(spectra.shape, jnp.bfloat16),
        ],
        scratch_shapes=[
            pltpu.SMEM(sources.shape, jnp.int32),
            pltpu.VMEM(quality.shape, jnp.int32),
            pltpu.SemaphoreType.DMA((steps,)),
            pltpu.SemaphoreType.DMA((2,)),
        ],
        compiler_params=pltpu.CompilerParams(vmem_limit_bytes=16 * MIB),
        cost_estimate=COST,
        name="pick_sources",
    )(*(pltpu.with_memory_space_constraint(value, pltpu.HBM) for value in (sources, spectra, quality)))


def whiten_kernel(data_ref, scale_ref, after_ref, out_ref):
    _, window_count, freq_count, _ = data_ref.shape
    step = freq_count // 5
    for window in range(window_count):
        scale = scale_ref[window : window + 1, :]

        def apply(i, carry):
            bins = pl.ds(pl.multiple_of(i * step, step), step)
            for part in range(2):
                value = data_ref[part, window, bins, :].astype(jnp.float32) * scale
                out_ref[part, window, bins, :] = value.astype(jnp.bfloat16)
            return carry

        lax.fori_loop(0, freq_count // step, apply, 0)


def whiten(data, scale, after):
    return pl.pallas_call(
        whiten_kernel,
        in_specs=[VMEM, VMEM, ANY],
        out_specs=VMEM,
        out_shape=jax.ShapeDtypeStruct(data.shape, jnp.bfloat16),
        compiler_params=pltpu.CompilerParams(vmem_limit_bytes=16 * MIB),
        cost_estimate=COST,
        name="whiten_receivers",
    )(data, scale, after)


def add_kernel(count, *refs):
    total = refs[0][...].astype(jnp.float32)
    for ref in refs[1:count]:
        total = total + ref[...].astype(jnp.float32)
    refs[-1][...] = total.astype(refs[-1].dtype)


def add_after(after, *values):
    return pl.pallas_call(
        functools.partial(add_kernel, len(values)),
        in_specs=[VMEM] * len(values) + [ANY],
        out_specs=VMEM,
        out_shape=jax.ShapeDtypeStruct(values[0].shape, values[0].dtype),
        compiler_params=pltpu.CompilerParams(vmem_limit_bytes=16 * MIB),
        cost_estimate=COST,
        name="add",
    )(*values, after)


def table_kernel(after_ref, out_ref):
    lag_count, columns = out_ref.shape
    freq_count = columns // 2
    highs = lag_count // GROUP

    def angle(count, lag_of, offset):
        lag = lag_of(lax.broadcasted_iota(jnp.int32, (count, columns), 0)).astype(jnp.float32)
        column = lax.broadcasted_iota(jnp.int32, (count, columns), 1).astype(jnp.float32)
        part = (column >= freq_count).astype(jnp.float32)
        turns = (column - part * freq_count + 1.0) * lag + part * offset
        turns = turns - columns * jnp.round(turns * (1.0 / columns))
        return turns * (math.pi / freq_count)

    high = angle(highs, lambda row: row * GROUP - lag_count // 2, freq_count // 2)
    low = angle(GROUP, lambda row: row, 0)
    cos_high, sin_high = jnp.cos(high), jnp.sin(high)
    cos_low, sin_low = jnp.cos(low) / freq_count, jnp.sin(low) / freq_count
    for row in range(highs):
        value = cos_high[row : row + 1] * cos_low - sin_high[row : row + 1] * sin_low
        out_ref[row * GROUP : (row + 1) * GROUP, :] = value.astype(jnp.bfloat16)


def lag_table(freq_count, lag_count, after):
    return pl.pallas_call(
        table_kernel,
        in_specs=[ANY],
        out_specs=VMEM,
        out_shape=jax.ShapeDtypeStruct((lag_count, 2 * freq_count), jnp.bfloat16),
        compiler_params=pltpu.CompilerParams(vmem_limit_bytes=16 * MIB),
        cost_estimate=COST,
        name="lag_table",
    )(after)


def lags_kernel(base, done, hours, *refs):
    hour = lax.axis_index("hour")
    here = functools.reduce(jnp.logical_or, [hour == value for value in hours])

    @pl.when(here)
    def _():
        make_lags(base, done, *refs)


def make_lags(base, done, own_ref, other_ref, receivers_ref, table_ref, after_ref, out_ref, *refs):
    spec_ref, cross_ref = refs[-2:]
    count = 8
    _, window_count, freq_count, channels_here = receivers_ref.shape
    wide = own_ref.shape[1]
    groups = freq_count // GROUP
    even = (lax.axis_index("chan") % 2) == 0

    def load(i):
        rows = pl.ds(pl.multiple_of(base + i * 16, 16), 16)
        own = own_ref[rows, :].astype(jnp.float32)
        other = other_ref[rows, :].astype(jnp.float32)
        return jnp.where(even, own, other), jnp.where(even, other, own)

    def add(i, total):
        real, imag = load(i)
        square = real * real + imag * imag
        return total + square[:8] + square[8:]

    total = lax.fori_loop(0, groups // 2, add, jnp.zeros((8, wide), jnp.float32), unroll=5)
    same = (
        lax.broadcasted_iota(jnp.int32, (wide, wide), 0) // GROUP
        == lax.broadcasted_iota(jnp.int32, (wide, wide), 1) // GROUP
    ).astype(jnp.float32)
    power = jnp.dot(total, same, preferred_element_type=jnp.float32, precision=lax.Precision.HIGHEST)
    scale = lax.rsqrt(power / freq_count + 1e-06)
    scale = jnp.concatenate([scale, scale], 0)

    def apply(i, carry):
        rows = pl.ds(pl.multiple_of(i * 16, 16), 16)
        for part, value in enumerate(load(i)):
            spec_ref[part, rows, :] = (value * scale).astype(jnp.bfloat16).astype(jnp.float32)
        return carry

    lax.fori_loop(0, groups // 2, apply, 0, unroll=5)

    diagonal = [
        lax.broadcasted_iota(jnp.int32, (8, wide), 1) % GROUP
        == lax.broadcasted_iota(jnp.int32, (8, wide), 0) + low
        for low in (0, 8)
    ]
    zero = jnp.zeros((8, wide), jnp.float32)

    def cross_of(group, carry):
        tiles = []
        for part in range(2):
            rows = spec_ref[part, pl.ds(pl.multiple_of(group * 8, 8), 8), :]
            for at in range(count):
                row = jnp.broadcast_to(rows[at : at + 1, :], (8, wide))
                tiles += [jnp.where(mask, row, zero) for mask in diagonal]
        bins = pl.ds(pl.multiple_of(group * GROUP, GROUP), GROUP)
        real = receivers_ref[0, :, bins, :].reshape(wide, channels_here)
        imag = receivers_ref[1, :, bins, :].reshape(wide, channels_here)
        cross = jnp.dot(
            jnp.concatenate(tiles, 0).astype(jnp.bfloat16),
            jnp.concatenate([real, imag], 1),
            preferred_element_type=jnp.float32,
        )
        half = count * GROUP
        parts = (
            cross[:half, :channels_here] + cross[half:, channels_here:],
            cross[:half, channels_here:] - cross[half:, :channels_here],
        )
        for part, value in enumerate(parts):
            value = value.astype(jnp.bfloat16)
            rows = pl.ds(pl.multiple_of(part * freq_count + group * GROUP, GROUP), GROUP)
            for at in range(count):
                ref, pair = (cross_ref, at // 2) if at < done else (refs[0], (at - done) // 2)
                lanes = slice((at % 2) * channels_here, (at % 2 + 1) * channels_here)
                ref[pair, rows, lanes] = value[at * GROUP : (at + 1) * GROUP]
        return carry

    lax.fori_loop(0, groups, cross_of, 0, unroll=25)
    transform(cross_ref, table_ref, out_ref)


def transform(cross_ref, table_ref, out_ref):
    channels_here = out_ref.shape[2]
    rows = 128
    for pair in range(cross_ref.shape[0]):
        for block in range(table_ref.shape[0] // rows):
            lags = slice(block * rows, (block + 1) * rows)
            value = jnp.dot(
                table_ref[lags, :], cross_ref[pair], preferred_element_type=jnp.float32
            ).astype(jnp.bfloat16)
            out_ref[2 * pair, lags, :] = value[:, :channels_here]
            out_ref[2 * pair + 1, lags, :] = value[:, channels_here:]


def lags_of(own, other, receivers, table, base, done, hours, after):
    _, window_count, freq_count, channels_here = receivers.shape
    wide = own.shape[1]
    count = 8
    cross = lambda sources: (sources // 2, 2 * freq_count, 2 * channels_here)
    out_shape = [jax.ShapeDtypeStruct((done, table.shape[0], channels_here), jnp.bfloat16)]
    if done < count:
        out_shape.append(jax.ShapeDtypeStruct(cross(count - done), jnp.bfloat16))
    return pl.pallas_call(
        functools.partial(lags_kernel, base, done, hours),
        in_specs=[VMEM] * 4 + [ANY],
        out_specs=[VMEM] * len(out_shape),
        out_shape=out_shape,
        scratch_shapes=[
            pltpu.VMEM((2, freq_count // GROUP * 8, wide), jnp.float32),
            pltpu.VMEM(cross(done), jnp.bfloat16),
        ],
        compiler_params=pltpu.CompilerParams(vmem_limit_bytes=16 * MIB),
        cost_estimate=COST,
        name="lags",
    )(own, other, receivers, table, after)


def lags_of_rest(cross, table, after):
    pairs, _, lanes = cross.shape
    return pl.pallas_call(
        lambda cross_ref, table_ref, after_ref, out_ref: transform(cross_ref, table_ref, out_ref),
        in_specs=[VMEM, VMEM, ANY],
        out_specs=VMEM,
        out_shape=jax.ShapeDtypeStruct((2 * pairs, table.shape[0], lanes // 2), jnp.bfloat16),
        compiler_params=pltpu.CompilerParams(vmem_limit_bytes=16 * MIB),
        cost_estimate=COST,
        name="lags_rest",
    )(cross, table, after)


def sum_kernel(firsts, low, *refs):
    out_ref, rest = refs[len(firsts) + 1], refs[len(firsts) + 2 :]
    total_ref = rest[0] if rest else out_ref
    copies = []
    for source in range(low, low + out_ref.shape[0]):
        total = 0.0
        for first, ref in zip(firsts, refs):
            if first <= source < first + ref.shape[0]:
                total = total + ref[source - first].astype(jnp.float32)
        total_ref[source - low] = total.astype(total_ref.dtype)
        if rest:
            copies.append(
                pltpu.make_async_copy(total_ref.at[source], out_ref.at[source], rest[1].at[source])
            )
            copies[-1].start()
    for copy in copies:
        copy.wait()


def sum_of(parts, low, high, dtype, after, final=False):
    firsts, values = zip(*parts)
    shape = (high - low,) + values[0].shape[1:]
    scratch = [pltpu.VMEM(shape, dtype), pltpu.SemaphoreType.DMA((high - low,))]
    return pl.pallas_call(
        functools.partial(sum_kernel, firsts, low),
        in_specs=[VMEM] * len(values) + [ANY],
        out_specs=HBM if final else VMEM,
        out_shape=jax.ShapeDtypeStruct(shape, dtype),
        scratch_shapes=scratch if final else [],
        compiler_params=pltpu.CompilerParams(vmem_limit_bytes=16 * MIB),
        cost_estimate=COST,
        name="sum",
    )(*values, after)


def chip_stages(chan_count):
    bits = [1 << b for b in range(1, chan_count.bit_length() - 1)]
    turned = bits[1:] + bits[:1]
    return [
        [(i, i ^ (odd_bit if i % 2 else even_bit)) for i in range(chan_count)]
        for even_bit, odd_bit in zip(bits, turned)
    ]


def body(chan_count, spectra, quality, sources):
    freq_count = spectra.shape[2]
    stages = chip_stages(chan_count)
    cores = [(i, i ^ 1) for i in range(chan_count)]
    over_chan = lambda value, pairs: lax.ppermute(value, "chan", pairs)
    over_hour = lambda value, pairs: lax.ppermute(value, "hour", pairs)

    front_out = front(spectra, quality, sources)
    (*state, scale, data) = front_out[:3] + front_out[6:]
    slot_rows = state[0].shape[0]
    moved = [over_chan(value, cores) for value in front_out[3:6]]
    passes = [0, 0, 0]
    made, mine, cross, middle, outward = {}, {}, {}, {}, {}
    inward = {}
    cuts = (0, SPLITS[0], 8)
    last = scale
    for step in STEPS:
        kind, at = step[0], int(step[1:] or 0)
        if kind == "r":
            for pairs in (stages[:1], stages[1:], [cores])[passes[at]]:
                last = state[at] = add_after(last, state[at], moved[at])
                moved[at] = over_chan(last, pairs)
            passes[at] += 1
        elif kind == "t":
            table = last = lag_table(freq_count, LAGS, last)
        elif kind == "w":
            receivers = last = whiten(data, scale, last)
        elif kind in "li":
            chunk = min(at, 2)
            first, hours = SPLITS[at], (0, 1, 2, 3)
            if at == 0:
                first, hours = (first, ENDS) if kind == "l" else (8, INNER)
            base = slot_rows * (at - chunk)
            values = lags_of(state[chunk], moved[chunk], receivers, table, base, first, hours, last)
            last = mine[at, kind] = values[0]
            if kind == "l":
                cross[at] = values[-1]
                if at < 3:
                    inward[at, kind] = over_hour(last, INWARD)
        elif kind == "k":
            last = mine[at, kind] = lags_of_rest(cross[at], table, last)
            inward[at, kind] = over_hour(last, INWARD)
        elif kind in "mn":
            which, low = ("l", 0) if kind == "m" else ("k", SPLITS[at])
            part = (0, mine[0, "i"]) if at == 0 else (low, mine[at, which])
            high = low + inward[at, which].shape[0]
            last = sum_of([part, (low, inward[at, which])], low, high, jnp.bfloat16, last)
            middle[at, which] = over_hour(last, MIDDLE)
        elif kind in "fg":
            which, part = ("l", 0) if kind == "f" else ("k", 1)
            parts = [(0, mine[2, "l"]), (cuts[part], middle[0, which])]
            last = sum_of(parts, cuts[part], cuts[part + 1], jnp.bfloat16, last)
            outward[which] = over_hour(last, OUTWARD)
        elif kind == "h":
            parts = [(0, mine[3, "l"]), (0, outward["l"]), (0, middle[1, "l"])]
            early = last = sum_of(parts, 0, cuts[1], jnp.float32, last)
        elif kind == "p":
            parts = [(0, early), (cuts[1], mine[3, "l"][cuts[1] :]), (cuts[1], outward["k"])]
            parts += [(SPLITS[1], middle[1, "k"])]
            last = sum_of(parts, 0, 8, jnp.float32, last)
    return sum_of([(0, last), (0, inward[2, "l"])], 0, 8, jnp.bfloat16, last, final=True)


def solution(mesh):
    placed = (P(None, "hour", None, "chan"), P("hour", "chan"), P())
    return jax.shard_map(
        functools.partial(body, mesh.shape["chan"]),
        mesh=mesh,
        in_specs=placed,
        out_specs=P("hour", None, "chan"),
        check_vma=False,
    )
```

```python
import functools
import math

import jax
import jax.numpy as jnp
from jax import lax
from jax.experimental import pallas as pl
from jax.experimental.pallas import tpu as pltpu
from jax.sharding import PartitionSpec as P

LAGS = 512
GROUP = 16
ORDER = ((3, 2, 1, 0), (3, 2, 0, 1), (0, 1, 3, 2), (0, 1, 2, 3))
SPLITS = (4, 2, 8, 8)
STEPS = (
    "r0", "r1", "t", "r0", "w", "r1", "r2", "r0", "l0", "k0",
    "i0", "r1", "r2", "l1", "m0", "r2", "k1", "n0", "l2", "m1", "f", "l3", "g", "h", "n1", "p",
)
INWARD = ((0, 1), (3, 2))
MIDDLE = ((1, 2), (2, 1))
OUTWARD = ((1, 0), (2, 3))
ENDS, INNER = (0, 3), (1, 2)
MIB = 1024 * 1024
COST = pl.CostEstimate(flops=1, bytes_accessed=1, transcendentals=0)

HBM = pl.BlockSpec(memory_space=pltpu.HBM)
ANY = pl.BlockSpec(memory_space=pl.ANY)
VMEM = pl.BlockSpec(memory_space=pltpu.VMEM)


def quarter_of(hour, slot):
    quarter = jnp.int32(ORDER[0][slot])
    for row in range(1, 4):
        quarter = jnp.where(hour == row, jnp.int32(ORDER[row][slot]), quarter)
    return quarter


def shares(window_count, freq_count):
    middle = (freq_count // (2 * GROUP) + 1) // 2 * 2 * GROUP
    half = window_count // 2
    return [
        ((low, low + half), bins) for low in (0, half) for bins in ((0, middle), (middle, freq_count))
    ]


def front_kernel(
    sources_hbm, spectra_hbm, quality_hbm,
    own_first_ref, own_second_ref, own_rest_ref, other_first_ref, other_second_ref, other_rest_ref,
    scale_ref, data_ref,
    sources_ref, quality_ref, sems, small_sems,
):
    small = [
        pltpu.make_async_copy(sources_hbm, sources_ref, small_sems.at[0]),
        pltpu.make_async_copy(quality_hbm, quality_ref, small_sems.at[1]),
    ]
    _, window_count, freq_count, channels_here = data_ref.shape
    large = []
    for at, (windows, bins) in enumerate(shares(window_count, freq_count)):
        part = (slice(None), pl.ds(windows[0], windows[1] - windows[0]), pl.ds(bins[0], bins[1] - bins[0]))
        large.append(pltpu.make_async_copy(spectra_hbm.at[part], data_ref.at[part], sems.at[at]))
    for copy in small + large:
        copy.start()
    source_count = sources_ref.shape[0]
    per_slot = source_count // 4
    wide = window_count * GROUP
    chan = lax.axis_index("chan")
    hour = lax.axis_index("hour")
    even = (chan % 2) == 0
    for copy in small:
        copy.wait()
    row = lax.broadcasted_iota(jnp.int32, (source_count, channels_here), 0)
    lane = lax.broadcasted_iota(jnp.int32, (source_count, channels_here), 1)
    wanted = jnp.full((source_count, channels_here), -1, jnp.int32)
    for slot in range(4):
        first = quarter_of(hour, slot) * per_slot
        for at in range(per_slot):
            wanted = jnp.where(row == slot * per_slot + at, sources_ref[first + at], wanted)
    onehot = (wanted - chan * channels_here == lane).astype(jnp.float32).astype(jnp.bfloat16)
    quality = quality_ref[...].astype(jnp.float32)
    usable = lax.dot_general(
        onehot, quality.astype(jnp.bfloat16), (((1,), (1,)), ((), ())), preferred_element_type=jnp.float32
    )
    spread = (
        lax.broadcasted_iota(jnp.int32, (window_count, wide), 1) // GROUP
        == lax.broadcasted_iota(jnp.int32, (window_count, wide), 0)
    )
    usable = jnp.dot(
        usable.astype(jnp.bfloat16),
        spread.astype(jnp.float32).astype(jnp.bfloat16),
        preferred_element_type=jnp.float32,
    )
    narrow = wide // 2
    totals = {}
    for copy, (windows, bins) in zip(large, shares(window_count, freq_count)):
        copy.wait()
        lanes = slice(windows[0] * GROUP, windows[1] * GROUP)
        usable_here = jnp.concatenate([usable[:, lanes]] * 2, 1)
        total = totals.get(windows, jnp.zeros((windows[1] - windows[0], 8, channels_here), jnp.float32))
        for pair in range(bins[0] // (2 * GROUP), bins[1] // (2 * GROUP)):
            picked = []
            for part in range(2):
                both = []
                for group in (2 * pair, 2 * pair + 1):
                    columns = data_ref[
                        part, windows[0] : windows[1], group * GROUP : (group + 1) * GROUP, :
                    ]
                    value = columns.astype(jnp.float32)
                    square = value * value
                    total = total + (square[:, :8] + square[:, 8:])
                    both.append(columns.reshape(narrow, channels_here))
                picked.append(
                    lax.dot_general(
                        onehot,
                        jnp.concatenate(both, 0),
                        (((1,), (1,)), ((), ())),
                        preferred_element_type=jnp.float32,
                    )
                    * usable_here
                )
            own = jnp.where(even, picked[0], picked[1])
            other = jnp.where(even, picked[1], picked[0])
            for value, first_ref, second_ref, rest_ref in (
                (own, own_first_ref, own_second_ref, own_rest_ref),
                (other, other_first_ref, other_second_ref, other_rest_ref),
            ):
                for slot, ref in enumerate((first_ref, second_ref, rest_ref, rest_ref)):
                    rows = slice(slot * per_slot, (slot + 1) * per_slot)
                    at = pair * 16 + max(slot - 2, 0) * freq_count // GROUP * per_slot
                    both = jnp.concatenate([value[rows, :narrow], value[rows, narrow:]], 0)
                    ref[at : at + 16, lanes] = both.astype(jnp.bfloat16)
        totals[windows] = total
    power = jnp.concatenate([jnp.sum(total, axis=1) for total in totals.values()], 0) / freq_count
    scale_ref[...] = lax.rsqrt(power + 1e-06) * quality


def front(spectra, quality, sources):
    _, window_count, freq_count, channels_here = spectra.shape
    rows = freq_count // GROUP * sources.shape[0] // 4
    wide = window_count * GROUP
    steps = len(shares(window_count, freq_count))
    shape = lambda count: jax.ShapeDtypeStruct((count * rows, wide), jnp.bfloat16)
    return pl.pallas_call(
        front_kernel,
        in_specs=[HBM, HBM, HBM],
        out_specs=[VMEM] * 8,
        out_shape=[
            *(shape(slots) for slots in (1, 1, 2) * 2),
            jax.ShapeDtypeStruct(quality.shape, jnp.float32),
            jax.ShapeDtypeStruct(spectra.shape, jnp.bfloat16),
        ],
        scratch_shapes=[
            pltpu.SMEM(sources.shape, jnp.int32),
            pltpu.VMEM(quality.shape, jnp.int32),
            pltpu.SemaphoreType.DMA((steps,)),
            pltpu.SemaphoreType.DMA((2,)),
        ],
        compiler_params=pltpu.CompilerParams(vmem_limit_bytes=16 * MIB),
        cost_estimate=COST,
        name="pick_sources",
    )(*(pltpu.with_memory_space_constraint(value, pltpu.HBM) for value in (sources, spectra, quality)))


def whiten_kernel(data_ref, scale_ref, after_ref, out_ref):
    _, window_count, freq_count, _ = data_ref.shape
    step = freq_count // 5
    for window in range(window_count):
        scale = scale_ref[window : window + 1, :]

        def apply(i, carry):
            bins = pl.ds(pl.multiple_of(i * step, step), step)
            for part in range(2):
                value = data_ref[part, window, bins, :].astype(jnp.float32) * scale
                out_ref[part, window, bins, :] = value.astype(jnp.bfloat16)
            return carry

        lax.fori_loop(0, freq_count // step, apply, 0)


def whiten(data, scale, after):
    return pl.pallas_call(
        whiten_kernel,
        in_specs=[VMEM, VMEM, ANY],
        out_specs=VMEM,
        out_shape=jax.ShapeDtypeStruct(data.shape, jnp.bfloat16),
        compiler_params=pltpu.CompilerParams(vmem_limit_bytes=16 * MIB),
        cost_estimate=COST,
        name="whiten_receivers",
    )(data, scale, after)


def add_kernel(count, *refs):
    total = refs[0][...].astype(jnp.float32)
    for ref in refs[1:count]:
        total = total + ref[...].astype(jnp.float32)
    refs[-1][...] = total.astype(refs[-1].dtype)


def add_after(after, *values):
    return pl.pallas_call(
        functools.partial(add_kernel, len(values)),
        in_specs=[VMEM] * len(values) + [ANY],
        out_specs=VMEM,
        out_shape=jax.ShapeDtypeStruct(values[0].shape, values[0].dtype),
        compiler_params=pltpu.CompilerParams(vmem_limit_bytes=16 * MIB),
        cost_estimate=COST,
        name="add",
    )(*values, after)


def table_kernel(after_ref, out_ref):
    lag_count, columns = out_ref.shape
    freq_count = columns // 2
    highs = lag_count // GROUP

    def angle(count, lag_of, offset):
        lag = lag_of(lax.broadcasted_iota(jnp.int32, (count, columns), 0)).astype(jnp.float32)
        column = lax.broadcasted_iota(jnp.int32, (count, columns), 1).astype(jnp.float32)
        part = (column >= freq_count).astype(jnp.float32)
        turns = (column - part * freq_count + 1.0) * lag + part * offset
        turns = turns - columns * jnp.round(turns * (1.0 / columns))
        return turns * (math.pi / freq_count)

    high = angle(highs, lambda row: row * GROUP - lag_count // 2, freq_count // 2)
    low = angle(GROUP, lambda row: row, 0)
    cos_high, sin_high = jnp.cos(high), jnp.sin(high)
    cos_low, sin_low = jnp.cos(low) / freq_count, jnp.sin(low) / freq_count
    for row in range(highs):
        value = cos_high[row : row + 1] * cos_low - sin_high[row : row + 1] * sin_low
        out_ref[row * GROUP : (row + 1) * GROUP, :] = value.astype(jnp.bfloat16)


def lag_table(freq_count, lag_count, after):
    return pl.pallas_call(
        table_kernel,
        in_specs=[ANY],
        out_specs=VMEM,
        out_shape=jax.ShapeDtypeStruct((lag_count, 2 * freq_count), jnp.bfloat16),
        compiler_params=pltpu.CompilerParams(vmem_limit_bytes=16 * MIB),
        cost_estimate=COST,
        name="lag_table",
    )(after)


def lags_kernel(base, sources, done, hours, *refs):
    hour = lax.axis_index("hour")
    here = functools.reduce(jnp.logical_or, [hour == value for value in hours])

    @pl.when(here)
    def _():
        make_lags(base, sources, done, *refs)


def make_lags(base, sources, done, own_ref, other_ref, receivers_ref, table_ref, after_ref, out_ref, *refs):
    spec_ref, cross_ref = refs[-2:]
    count = len(sources)
    _, window_count, freq_count, channels_here = receivers_ref.shape
    wide = own_ref.shape[1]
    groups = freq_count // GROUP
    even = (lax.axis_index("chan") % 2) == 0

    def load(i):
        rows = pl.ds(pl.multiple_of(base + i * 16, 16), 16)
        own = own_ref[rows, :].astype(jnp.float32)
        other = other_ref[rows, :].astype(jnp.float32)
        return jnp.where(even, own, other), jnp.where(even, other, own)

    def add(i, total):
        real, imag = load(i)
        square = real * real + imag * imag
        return total + square[:8] + square[8:]

    total = lax.fori_loop(0, groups // 2, add, jnp.zeros((8, wide), jnp.float32), unroll=groups // 2)
    same = (
        lax.broadcasted_iota(jnp.int32, (wide, wide), 0) // GROUP
        == lax.broadcasted_iota(jnp.int32, (wide, wide), 1) // GROUP
    ).astype(jnp.float32)
    power = jnp.dot(total, same, preferred_element_type=jnp.float32, precision=lax.Precision.HIGHEST)
    scale = lax.rsqrt(power / freq_count + 1e-06)
    scale = jnp.concatenate([scale, scale], 0)

    def apply(i, carry):
        rows = pl.ds(pl.multiple_of(i * 16, 16), 16)
        for part, value in enumerate(load(i)):
            spec_ref[part, rows, :] = (value * scale).astype(jnp.bfloat16).astype(jnp.float32)
        return carry

    lax.fori_loop(0, groups // 2, apply, 0, unroll=groups // 2)

    diagonal = [
        lax.broadcasted_iota(jnp.int32, (8, wide), 1) % GROUP
        == lax.broadcasted_iota(jnp.int32, (8, wide), 0) + low
        for low in (0, 8)
    ]
    zero = jnp.zeros((8, wide), jnp.float32)

    def cross_of(group, carry):
        tiles = []
        for part in range(2):
            rows = spec_ref[part, pl.ds(pl.multiple_of(group * 8, 8), 8), :]
            for at in sources:
                row = jnp.broadcast_to(rows[at : at + 1, :], (8, wide))
                tiles += [jnp.where(mask, row, zero) for mask in diagonal]
        bins = pl.ds(pl.multiple_of(group * GROUP, GROUP), GROUP)
        real = receivers_ref[0, :, bins, :].reshape(wide, channels_here)
        imag = receivers_ref[1, :, bins, :].reshape(wide, channels_here)
        cross = jnp.dot(
            jnp.concatenate(tiles, 0).astype(jnp.bfloat16),
            jnp.concatenate([real, imag], 1),
            preferred_element_type=jnp.float32,
        )
        half = count * GROUP
        parts = (
            cross[:half, :channels_here] + cross[half:, channels_here:],
            cross[:half, channels_here:] - cross[half:, :channels_here],
        )
        for part, value in enumerate(parts):
            value = value.astype(jnp.bfloat16)
            rows = pl.ds(pl.multiple_of(part * freq_count + group * GROUP, GROUP), GROUP)
            for at in range(count):
                ref, pair = (cross_ref, at // 2) if at < done else (refs[0], (at - done) // 2)
                lanes = slice((at % 2) * channels_here, (at % 2 + 1) * channels_here)
                ref[pair, rows, lanes] = value[at * GROUP : (at + 1) * GROUP]
        return carry

    lax.fori_loop(0, groups, cross_of, 0, unroll=groups)
    transform(cross_ref, table_ref, out_ref)


def transform(cross_ref, table_ref, out_ref):
    channels_here = out_ref.shape[2]
    rows = 128
    for pair in range(cross_ref.shape[0]):
        for block in range(table_ref.shape[0] // rows):
            lags = slice(block * rows, (block + 1) * rows)
            value = jnp.dot(
                table_ref[lags, :], cross_ref[pair], preferred_element_type=jnp.float32
            ).astype(jnp.bfloat16)
            out_ref[2 * pair, lags, :] = value[:, :channels_here]
            out_ref[2 * pair + 1, lags, :] = value[:, channels_here:]


def lags_of(own, other, receivers, table, base, sources, done, hours, after):
    _, window_count, freq_count, channels_here = receivers.shape
    wide = own.shape[1]
    count = len(sources)
    cross = lambda some: (some // 2, 2 * freq_count, 2 * channels_here)
    out_shape = [jax.ShapeDtypeStruct((done, table.shape[0], channels_here), jnp.bfloat16)]
    if done < count:
        out_shape.append(jax.ShapeDtypeStruct(cross(count - done), jnp.bfloat16))
    return pl.pallas_call(
        functools.partial(lags_kernel, base, sources, done, hours),
        in_specs=[VMEM] * 4 + [ANY],
        out_specs=[VMEM] * len(out_shape),
        out_shape=out_shape,
        scratch_shapes=[
            pltpu.VMEM((2, freq_count // GROUP * 8, wide), jnp.float32),
            pltpu.VMEM(cross(done), jnp.bfloat16),
        ],
        compiler_params=pltpu.CompilerParams(vmem_limit_bytes=16 * MIB),
        cost_estimate=COST,
        name="lags",
    )(own, other, receivers, table, after)


def lags_of_rest(cross, table, after):
    pairs, _, lanes = cross.shape
    return pl.pallas_call(
        lambda cross_ref, table_ref, after_ref, out_ref: transform(cross_ref, table_ref, out_ref),
        in_specs=[VMEM, VMEM, ANY],
        out_specs=VMEM,
        out_shape=jax.ShapeDtypeStruct((2 * pairs, table.shape[0], lanes // 2), jnp.bfloat16),
        compiler_params=pltpu.CompilerParams(vmem_limit_bytes=16 * MIB),
        cost_estimate=COST,
        name="lags_rest",
    )(cross, table, after)


def sum_kernel(firsts, low, *refs):
    out_ref, rest = refs[len(firsts) + 1], refs[len(firsts) + 2 :]
    total_ref = rest[0] if rest else out_ref
    copies = []
    for source in range(low, low + out_ref.shape[0]):
        total = 0.0
        for first, ref in zip(firsts, refs):
            if first <= source < first + ref.shape[0]:
                total = total + ref[source - first].astype(jnp.float32)
        total_ref[source - low] = total.astype(total_ref.dtype)
        if rest:
            copies.append(
                pltpu.make_async_copy(total_ref.at[source], out_ref.at[source], rest[1].at[source])
            )
            copies[-1].start()
    for copy in copies:
        copy.wait()


def sum_of(parts, low, high, dtype, after, final=False):
    firsts, values = zip(*parts)
    shape = (high - low,) + values[0].shape[1:]
    scratch = [pltpu.VMEM(shape, dtype), pltpu.SemaphoreType.DMA((high - low,))]
    return pl.pallas_call(
        functools.partial(sum_kernel, firsts, low),
        in_specs=[VMEM] * len(values) + [ANY],
        out_specs=HBM if final else VMEM,
        out_shape=jax.ShapeDtypeStruct(shape, dtype),
        scratch_shapes=scratch if final else [],
        compiler_params=pltpu.CompilerParams(vmem_limit_bytes=16 * MIB),
        cost_estimate=COST,
        name="sum",
    )(*values, after)


def chip_stages(chan_count):
    bits = [1 << b for b in range(1, chan_count.bit_length() - 1)]
    turned = bits[1:] + bits[:1]
    return [
        [(i, i ^ (odd_bit if i % 2 else even_bit)) for i in range(chan_count)]
        for even_bit, odd_bit in zip(bits, turned)
    ]


def body(chan_count, spectra, quality, sources):
    freq_count = spectra.shape[2]
    stages = chip_stages(chan_count)
    cores = [(i, i ^ 1) for i in range(chan_count)]
    over_chan = lambda value, pairs: lax.ppermute(value, "chan", pairs)
    over_hour = lambda value, pairs: lax.ppermute(value, "hour", pairs)

    front_out = front(spectra, quality, sources)
    (*state, scale, data) = front_out[:3] + front_out[6:]
    slot_rows = state[0].shape[0]
    moved = [over_chan(value, cores) for value in front_out[3:6]]
    passes = [0, 0, 0]
    made, mine, cross, middle, outward = {}, {}, {}, {}, {}
    inward = {}
    cuts = (0, SPLITS[0], 8)
    last = scale
    for step in STEPS:
        kind, at = step[0], int(step[1:] or 0)
        if kind == "r":
            for pairs in (stages[:1], stages[1:], [cores])[passes[at]]:
                last = state[at] = add_after(last, state[at], moved[at])
                moved[at] = over_chan(last, pairs)
            passes[at] += 1
        elif kind == "t":
            table = last = lag_table(freq_count, LAGS, last)
        elif kind == "w":
            receivers = last = whiten(data, scale, last)
        elif kind in "li" or step == "k0":
            chunk = min(at, 2)
            some, first, hours = range(8), SPLITS[at], (0, 1, 2, 3)
            if at == 0:
                some = {"l": range(first), "k": range(first, 8), "i": range(8)}[kind]
                first, hours = len(some), INNER if kind == "i" else ENDS
            base = slot_rows * (at - chunk)
            values = lags_of(state[chunk], moved[chunk], receivers, table, base, some, first, hours, last)
            last = mine[at, kind] = values[0]
            cross[at] = values[-1]
            if kind != "i" and at < 3:
                inward[at, kind] = over_hour(last, INWARD)
        elif kind == "k":
            last = mine[at, kind] = lags_of_rest(cross[at], table, last)
            inward[at, kind] = over_hour(last, INWARD)
        elif kind in "mn":
            which, low = ("l", 0) if kind == "m" else ("k", SPLITS[at])
            part = (0, mine[0, "i"]) if at == 0 else (low, mine[at, which])
            high = low + inward[at, which].shape[0]
            last = sum_of([part, (low, inward[at, which])], low, high, jnp.bfloat16, last)
            middle[at, which] = over_hour(last, MIDDLE)
        elif kind in "fg":
            which, part = ("l", 0) if kind == "f" else ("k", 1)
            parts = [(0, mine[2, "l"]), (cuts[part], middle[0, which])]
            last = sum_of(parts, cuts[part], cuts[part + 1], jnp.bfloat16, last)
            outward[which] = over_hour(last, OUTWARD)
        elif kind == "h":
            parts = [(0, mine[3, "l"]), (0, outward["l"]), (0, middle[1, "l"])]
            early = last = sum_of(parts, 0, cuts[1], jnp.float32, last)
        elif kind == "p":
            parts = [(0, early), (cuts[1], mine[3, "l"][cuts[1] :]), (cuts[1], outward["k"])]
            parts += [(SPLITS[1], middle[1, "k"])]
            last = sum_of(parts, 0, 8, jnp.float32, last)
    return sum_of([(0, last), (0, inward[2, "l"])], 0, 8, jnp.bfloat16, last, final=True)


def solution(mesh):
    placed = (P(None, "hour", None, "chan"), P("hour", "chan"), P())
    return jax.shard_map(
        functools.partial(body, mesh.shape["chan"]),
        mesh=mesh,
        in_specs=placed,
        out_specs=P("hour", None, "chan"),
        check_vma=False,
    )
```

```python
import functools
import math

import jax
import jax.numpy as jnp
from jax import lax
from jax.experimental import pallas as pl
from jax.experimental.pallas import tpu as pltpu
from jax.sharding import PartitionSpec as P

LAGS = 512
GROUP = 16
ORDER = ((3, 2, 1, 0), (3, 2, 0, 1), (0, 1, 3, 2), (0, 1, 2, 3))
SPLITS = (4, 2, 8, 8)
STEPS = (
    "r0", "q", "r0", "w", "t", "r0", "r1", "r2", "l0", "r1", "k0",
    "i0", "r1", "r2", "l1", "m0", "r2", "k1", "n0", "l2", "m1", "f", "l3", "g", "h", "n1", "p",
)
INWARD = ((0, 1), (3, 2))
MIDDLE = ((1, 2), (2, 1))
OUTWARD = ((1, 0), (2, 3))
ENDS, INNER = (0, 3), (1, 2)
MIB = 1024 * 1024
COST = pl.CostEstimate(flops=1, bytes_accessed=1, transcendentals=0)

HBM = pl.BlockSpec(memory_space=pltpu.HBM)
ANY = pl.BlockSpec(memory_space=pl.ANY)
VMEM = pl.BlockSpec(memory_space=pltpu.VMEM)


def quarter_of(hour, slot):
    quarter = jnp.int32(ORDER[0][slot])
    for row in range(1, 4):
        quarter = jnp.where(hour == row, jnp.int32(ORDER[row][slot]), quarter)
    return quarter


def shares(window_count, freq_count):
    middle = (freq_count // (2 * GROUP) + 1) // 2 * 2 * GROUP
    half = window_count // 2
    return [
        ((low, low + half), bins) for low in (0, half) for bins in ((0, middle), (middle, freq_count))
    ]


def pick_share(data_ref, onehot, usable, windows, bins, own_refs, other_refs, total=None):
    channels_here = data_ref.shape[3]
    narrow = usable.shape[1] // 2
    per_slot = onehot.shape[0] // len(own_refs)
    lanes = slice(windows[0] * GROUP, windows[1] * GROUP)
    usable_here = jnp.concatenate([usable[:, lanes]] * 2, 1)
    even = (lax.axis_index("chan") % 2) == 0
    for pair in range(bins[0] // (2 * GROUP), bins[1] // (2 * GROUP)):
        picked = []
        for part in range(2):
            both = []
            for group in (2 * pair, 2 * pair + 1):
                columns = data_ref[part, windows[0] : windows[1], group * GROUP : (group + 1) * GROUP, :]
                if total is not None:
                    value = columns.astype(jnp.float32)
                    square = value * value
                    total = total + (square[:, :8] + square[:, 8:])
                both.append(columns.reshape(narrow, channels_here))
            picked.append(
                lax.dot_general(
                    onehot,
                    jnp.concatenate(both, 0),
                    (((1,), (1,)), ((), ())),
                    preferred_element_type=jnp.float32,
                )
                * usable_here
            )
        for refs, value in (
            (own_refs, jnp.where(even, picked[0], picked[1])),
            (other_refs, jnp.where(even, picked[1], picked[0])),
        ):
            for at, (ref, base) in enumerate(refs):
                rows = slice(at * per_slot, (at + 1) * per_slot)
                both = jnp.concatenate([value[rows, :narrow], value[rows, narrow:]], 0)
                ref[base + pair * 16 : base + pair * 16 + 16, lanes] = both.astype(jnp.bfloat16)
    return total


def front_kernel(
    sources_hbm, spectra_hbm, quality_hbm,
    own_ref, other_ref, data_ref, onehot_ref, usable_ref, quality_ref,
    sources_ref, flags_ref, sems, small_sems,
):
    small = [
        pltpu.make_async_copy(sources_hbm, sources_ref, small_sems.at[0]),
        pltpu.make_async_copy(quality_hbm, flags_ref, small_sems.at[1]),
    ]
    _, window_count, freq_count, channels_here = data_ref.shape
    large = []
    for at, (windows, bins) in enumerate(shares(window_count, freq_count)):
        part = (slice(None), pl.ds(windows[0], windows[1] - windows[0]), pl.ds(bins[0], bins[1] - bins[0]))
        large.append(pltpu.make_async_copy(spectra_hbm.at[part], data_ref.at[part], sems.at[at]))
    for copy in small + large:
        copy.start()
    source_count = sources_ref.shape[0]
    per_slot = source_count // 4
    wide = window_count * GROUP
    chan = lax.axis_index("chan")
    hour = lax.axis_index("hour")
    for copy in small:
        copy.wait()
    row = lax.broadcasted_iota(jnp.int32, (source_count, channels_here), 0)
    lane = lax.broadcasted_iota(jnp.int32, (source_count, channels_here), 1)
    wanted = jnp.full((source_count, channels_here), -1, jnp.int32)
    for slot in range(4):
        first = quarter_of(hour, slot) * per_slot
        for at in range(per_slot):
            wanted = jnp.where(row == slot * per_slot + at, sources_ref[first + at], wanted)
    onehot = (wanted - chan * channels_here == lane).astype(jnp.float32)
    quality = flags_ref[...].astype(jnp.float32)
    usable = lax.dot_general(
        onehot.astype(jnp.bfloat16),
        quality.astype(jnp.bfloat16),
        (((1,), (1,)), ((), ())),
        preferred_element_type=jnp.float32,
    )
    spread = (
        lax.broadcasted_iota(jnp.int32, (window_count, wide), 1) // GROUP
        == lax.broadcasted_iota(jnp.int32, (window_count, wide), 0)
    )
    usable = jnp.dot(
        usable.astype(jnp.bfloat16),
        spread.astype(jnp.float32).astype(jnp.bfloat16),
        preferred_element_type=jnp.float32,
    )
    onehot_ref[...] = onehot
    usable_ref[...] = usable
    quality_ref[...] = quality
    onehot = onehot[:per_slot].astype(jnp.bfloat16)
    for copy, (windows, bins) in zip(large, shares(window_count, freq_count)):
        copy.wait()
        pick_share(data_ref, onehot, usable[:per_slot], windows, bins, [(own_ref, 0)], [(other_ref, 0)])


def front(spectra, quality, sources):
    _, window_count, freq_count, channels_here = spectra.shape
    rows = freq_count // GROUP * sources.shape[0] // 4
    wide = window_count * GROUP
    steps = len(shares(window_count, freq_count))
    return pl.pallas_call(
        front_kernel,
        in_specs=[HBM, HBM, HBM],
        out_specs=[VMEM] * 6,
        out_shape=[
            jax.ShapeDtypeStruct((rows, wide), jnp.bfloat16),
            jax.ShapeDtypeStruct((rows, wide), jnp.bfloat16),
            jax.ShapeDtypeStruct(spectra.shape, jnp.bfloat16),
            jax.ShapeDtypeStruct((sources.shape[0], channels_here), jnp.float32),
            jax.ShapeDtypeStruct((sources.shape[0], wide), jnp.float32),
            jax.ShapeDtypeStruct(quality.shape, jnp.float32),
        ],
        scratch_shapes=[
            pltpu.SMEM(sources.shape, jnp.int32),
            pltpu.VMEM(quality.shape, jnp.int32),
            pltpu.SemaphoreType.DMA((steps,)),
            pltpu.SemaphoreType.DMA((2,)),
        ],
        compiler_params=pltpu.CompilerParams(vmem_limit_bytes=16 * MIB),
        cost_estimate=COST,
        name="pick_first",
    )(*(pltpu.with_memory_space_constraint(value, pltpu.HBM) for value in (sources, spectra, quality)))


def rest_kernel(
    data_ref, onehot_ref, usable_ref, quality_ref, after_ref,
    own_second_ref, own_rest_ref, other_second_ref, other_rest_ref, scale_ref,
):
    _, window_count, freq_count, channels_here = data_ref.shape
    rows = own_second_ref.shape[0]
    per_slot = onehot_ref.shape[0] // 4
    onehot = onehot_ref[per_slot:, :].astype(jnp.bfloat16)
    usable = usable_ref[per_slot:, :]
    own_refs = [(own_second_ref, 0), (own_rest_ref, 0), (own_rest_ref, rows)]
    other_refs = [(other_second_ref, 0), (other_rest_ref, 0), (other_rest_ref, rows)]
    totals = {}
    for windows, bins in shares(window_count, freq_count):
        total = totals.get(windows, jnp.zeros((windows[1] - windows[0], 8, channels_here), jnp.float32))
        totals[windows] = pick_share(data_ref, onehot, usable, windows, bins, own_refs, other_refs, total)
    power = jnp.concatenate([jnp.sum(total, axis=1) for total in totals.values()], 0) / freq_count
    scale_ref[...] = lax.rsqrt(power + 1e-06) * quality_ref[...]


def pick_rest(data, onehot, usable, quality, rows, after):
    shape = lambda slots: jax.ShapeDtypeStruct((slots * rows, usable.shape[1]), jnp.bfloat16)
    return pl.pallas_call(
        rest_kernel,
        in_specs=[VMEM] * 4 + [ANY],
        out_specs=[VMEM] * 5,
        out_shape=[shape(1), shape(2), shape(1), shape(2), jax.ShapeDtypeStruct(quality.shape, jnp.float32)],
        compiler_params=pltpu.CompilerParams(vmem_limit_bytes=16 * MIB),
        cost_estimate=COST,
        name="pick_rest",
    )(data, onehot, usable, quality, after)


def whiten_kernel(data_ref, scale_ref, after_ref, out_ref):
    _, window_count, freq_count, _ = data_ref.shape
    step = freq_count // 5
    for window in range(window_count):
        scale = scale_ref[window : window + 1, :]

        def apply(i, carry):
            bins = pl.ds(pl.multiple_of(i * step, step), step)
            for part in range(2):
                value = data_ref[part, window, bins, :].astype(jnp.float32) * scale
                out_ref[part, window, bins, :] = value.astype(jnp.bfloat16)
            return carry

        lax.fori_loop(0, freq_count // step, apply, 0)


def whiten(data, scale, after):
    return pl.pallas_call(
        whiten_kernel,
        in_specs=[VMEM, VMEM, ANY],
        out_specs=VMEM,
        out_shape=jax.ShapeDtypeStruct(data.shape, jnp.bfloat16),
        compiler_params=pltpu.CompilerParams(vmem_limit_bytes=16 * MIB),
        cost_estimate=COST,
        name="whiten_receivers",
    )(data, scale, after)


def add_kernel(count, *refs):
    total = refs[0][...].astype(jnp.float32)
    for ref in refs[1:count]:
        total = total + ref[...].astype(jnp.float32)
    refs[-1][...] = total.astype(refs[-1].dtype)


def add_after(after, *values):
    return pl.pallas_call(
        functools.partial(add_kernel, len(values)),
        in_specs=[VMEM] * len(values) + [ANY],
        out_specs=VMEM,
        out_shape=jax.ShapeDtypeStruct(values[0].shape, values[0].dtype),
        compiler_params=pltpu.CompilerParams(vmem_limit_bytes=16 * MIB),
        cost_estimate=COST,
        name="add",
    )(*values, after)


def table_kernel(after_ref, out_ref):
    lag_count, columns = out_ref.shape
    freq_count = columns // 2
    highs = lag_count // GROUP

    def angle(count, lag_of, offset):
        lag = lag_of(lax.broadcasted_iota(jnp.int32, (count, columns), 0)).astype(jnp.float32)
        column = lax.broadcasted_iota(jnp.int32, (count, columns), 1).astype(jnp.float32)
        part = (column >= freq_count).astype(jnp.float32)
        turns = (column - part * freq_count + 1.0) * lag + part * offset
        turns = turns - columns * jnp.round(turns * (1.0 / columns))
        return turns * (math.pi / freq_count)

    high = angle(highs, lambda row: row * GROUP - lag_count // 2, freq_count // 2)
    low = angle(GROUP, lambda row: row, 0)
    cos_high, sin_high = jnp.cos(high), jnp.sin(high)
    cos_low, sin_low = jnp.cos(low) / freq_count, jnp.sin(low) / freq_count
    for row in range(highs):
        value = cos_high[row : row + 1] * cos_low - sin_high[row : row + 1] * sin_low
        out_ref[row * GROUP : (row + 1) * GROUP, :] = value.astype(jnp.bfloat16)


def lag_table(freq_count, lag_count, after):
    return pl.pallas_call(
        table_kernel,
        in_specs=[ANY],
        out_specs=VMEM,
        out_shape=jax.ShapeDtypeStruct((lag_count, 2 * freq_count), jnp.bfloat16),
        compiler_params=pltpu.CompilerParams(vmem_limit_bytes=16 * MIB),
        cost_estimate=COST,
        name="lag_table",
    )(after)


def lags_kernel(base, sources, done, hours, *refs):
    hour = lax.axis_index("hour")
    here = functools.reduce(jnp.logical_or, [hour == value for value in hours])

    @pl.when(here)
    def _():
        make_lags(base, sources, done, *refs)


def make_lags(base, sources, done, own_ref, other_ref, receivers_ref, table_ref, after_ref, out_ref, *refs):
    spec_ref, cross_ref = refs[-2:]
    count = len(sources)
    _, window_count, freq_count, channels_here = receivers_ref.shape
    wide = own_ref.shape[1]
    groups = freq_count // GROUP
    even = (lax.axis_index("chan") % 2) == 0

    def load(i):
        rows = pl.ds(pl.multiple_of(base + i * 16, 16), 16)
        own = own_ref[rows, :].astype(jnp.float32)
        other = other_ref[rows, :].astype(jnp.float32)
        return jnp.where(even, own, other), jnp.where(even, other, own)

    def add(i, total):
        real, imag = load(i)
        square = real * real + imag * imag
        return total + square[:8] + square[8:]

    total = lax.fori_loop(0, groups // 2, add, jnp.zeros((8, wide), jnp.float32), unroll=groups // 2)
    same = (
        lax.broadcasted_iota(jnp.int32, (wide, wide), 0) // GROUP
        == lax.broadcasted_iota(jnp.int32, (wide, wide), 1) // GROUP
    ).astype(jnp.float32)
    power = jnp.dot(total, same, preferred_element_type=jnp.float32, precision=lax.Precision.HIGHEST)
    scale = lax.rsqrt(power / freq_count + 1e-06)
    scale = jnp.concatenate([scale, scale], 0)

    def apply(i, carry):
        rows = pl.ds(pl.multiple_of(i * 16, 16), 16)
        for part, value in enumerate(load(i)):
            spec_ref[part, rows, :] = (value * scale).astype(jnp.bfloat16).astype(jnp.float32)
        return carry

    lax.fori_loop(0, groups // 2, apply, 0, unroll=groups // 2)

    diagonal = [
        lax.broadcasted_iota(jnp.int32, (8, wide), 1) % GROUP
        == lax.broadcasted_iota(jnp.int32, (8, wide), 0) + low
        for low in (0, 8)
    ]
    zero = jnp.zeros((8, wide), jnp.float32)

    def cross_of(group, carry):
        tiles = []
        for part in range(2):
            rows = spec_ref[part, pl.ds(pl.multiple_of(group * 8, 8), 8), :]
            for at in sources:
                row = jnp.broadcast_to(rows[at : at + 1, :], (8, wide))
                tiles += [jnp.where(mask, row, zero) for mask in diagonal]
        bins = pl.ds(pl.multiple_of(group * GROUP, GROUP), GROUP)
        real = receivers_ref[0, :, bins, :].reshape(wide, channels_here)
        imag = receivers_ref[1, :, bins, :].reshape(wide, channels_here)
        cross = jnp.dot(
            jnp.concatenate(tiles, 0).astype(jnp.bfloat16),
            jnp.concatenate([real, imag], 1),
            preferred_element_type=jnp.float32,
        )
        half = count * GROUP
        parts = (
            cross[:half, :channels_here] + cross[half:, channels_here:],
            cross[:half, channels_here:] - cross[half:, :channels_here],
        )
        for part, value in enumerate(parts):
            value = value.astype(jnp.bfloat16)
            rows = pl.ds(pl.multiple_of(part * freq_count + group * GROUP, GROUP), GROUP)
            for at in range(count):
                ref, pair = (cross_ref, at // 2) if at < done else (refs[0], (at - done) // 2)
                lanes = slice((at % 2) * channels_here, (at % 2 + 1) * channels_here)
                ref[pair, rows, lanes] = value[at * GROUP : (at + 1) * GROUP]
        return carry

    lax.fori_loop(0, groups, cross_of, 0, unroll=groups)
    transform(cross_ref, table_ref, out_ref)


def transform(cross_ref, table_ref, out_ref):
    channels_here = out_ref.shape[2]
    rows = 128
    for pair in range(cross_ref.shape[0]):
        for block in range(table_ref.shape[0] // rows):
            lags = slice(block * rows, (block + 1) * rows)
            value = jnp.dot(
                table_ref[lags, :], cross_ref[pair], preferred_element_type=jnp.float32
            ).astype(jnp.bfloat16)
            out_ref[2 * pair, lags, :] = value[:, :channels_here]
            out_ref[2 * pair + 1, lags, :] = value[:, channels_here:]


def lags_of(own, other, receivers, table, base, sources, done, hours, after):
    _, window_count, freq_count, channels_here = receivers.shape
    wide = own.shape[1]
    count = len(sources)
    cross = lambda some: (some // 2, 2 * freq_count, 2 * channels_here)
    out_shape = [jax.ShapeDtypeStruct((done, table.shape[0], channels_here), jnp.bfloat16)]
    if done < count:
        out_shape.append(jax.ShapeDtypeStruct(cross(count - done), jnp.bfloat16))
    return pl.pallas_call(
        functools.partial(lags_kernel, base, sources, done, hours),
        in_specs=[VMEM] * 4 + [ANY],
        out_specs=[VMEM] * len(out_shape),
        out_shape=out_shape,
        scratch_shapes=[
            pltpu.VMEM((2, freq_count // GROUP * 8, wide), jnp.float32),
            pltpu.VMEM(cross(done), jnp.bfloat16),
        ],
        compiler_params=pltpu.CompilerParams(vmem_limit_bytes=16 * MIB),
        cost_estimate=COST,
        name="lags",
    )(own, other, receivers, table, after)


def lags_of_rest(cross, table, after):
    pairs, _, lanes = cross.shape
    return pl.pallas_call(
        lambda cross_ref, table_ref, after_ref, out_ref: transform(cross_ref, table_ref, out_ref),
        in_specs=[VMEM, VMEM, ANY],
        out_specs=VMEM,
        out_shape=jax.ShapeDtypeStruct((2 * pairs, table.shape[0], lanes // 2), jnp.bfloat16),
        compiler_params=pltpu.CompilerParams(vmem_limit_bytes=16 * MIB),
        cost_estimate=COST,
        name="lags_rest",
    )(cross, table, after)


def sum_kernel(firsts, low, *refs):
    out_ref, rest = refs[len(firsts) + 1], refs[len(firsts) + 2 :]
    total_ref = rest[0] if rest else out_ref
    copies = []
    for source in range(low, low + out_ref.shape[0]):
        total = 0.0
        for first, ref in zip(firsts, refs):
            if first <= source < first + ref.shape[0]:
                total = total + ref[source - first].astype(jnp.float32)
        total_ref[source - low] = total.astype(total_ref.dtype)
        if rest:
            copies.append(
                pltpu.make_async_copy(total_ref.at[source], out_ref.at[source], rest[1].at[source])
            )
            copies[-1].start()
    for copy in copies:
        copy.wait()


def sum_of(parts, low, high, dtype, after, final=False):
    firsts, values = zip(*parts)
    shape = (high - low,) + values[0].shape[1:]
    scratch = [pltpu.VMEM(shape, dtype), pltpu.SemaphoreType.DMA((high - low,))]
    return pl.pallas_call(
        functools.partial(sum_kernel, firsts, low),
        in_specs=[VMEM] * len(values) + [ANY],
        out_specs=HBM if final else VMEM,
        out_shape=jax.ShapeDtypeStruct(shape, dtype),
        scratch_shapes=scratch if final else [],
        compiler_params=pltpu.CompilerParams(vmem_limit_bytes=16 * MIB),
        cost_estimate=COST,
        name="sum",
    )(*values, after)


def chip_stages(chan_count):
    bits = [1 << b for b in range(1, chan_count.bit_length() - 1)]
    turned = bits[1:] + bits[:1]
    return [
        [(i, i ^ (odd_bit if i % 2 else even_bit)) for i in range(chan_count)]
        for even_bit, odd_bit in zip(bits, turned)
    ]


def body(chan_count, spectra, quality, sources):
    freq_count = spectra.shape[2]
    stages = chip_stages(chan_count)
    cores = [(i, i ^ 1) for i in range(chan_count)]
    over_chan = lambda value, pairs: lax.ppermute(value, "chan", pairs)
    over_hour = lambda value, pairs: lax.ppermute(value, "hour", pairs)

    own, other, data, onehot, usable, flags = front(spectra, quality, sources)
    slot_rows = own.shape[0]
    state = {0: own}
    moved = {0: over_chan(other, cores)}
    passes = [0, 0, 0]
    made, mine, cross, middle, outward = {}, {}, {}, {}, {}
    inward = {}
    cuts = (0, SPLITS[0], 8)
    last = onehot
    for step in STEPS:
        kind, at = step[0], int(step[1:] or 0)
        if kind == "r":
            for pairs in (stages[:1], stages[1:], [cores])[passes[at]]:
                last = state[at] = add_after(last, state[at], moved[at])
                moved[at] = over_chan(last, pairs)
            passes[at] += 1
        elif kind == "q":
            state[1], state[2], *others, scale = pick_rest(data, onehot, usable, flags, slot_rows, last)
            moved.update({1 + chunk: over_chan(value, cores) for chunk, value in enumerate(others)})
            last = scale
        elif kind == "t":
            table = last = lag_table(freq_count, LAGS, last)
        elif kind == "w":
            receivers = last = whiten(data, scale, last)
        elif kind in "li" or step == "k0":
            chunk = min(at, 2)
            some, first, hours = range(8), SPLITS[at], (0, 1, 2, 3)
            if at == 0:
                some = {"l": range(first), "k": range(first, 8), "i": range(8)}[kind]
                first, hours = len(some), INNER if kind == "i" else ENDS
            base = slot_rows * (at - chunk)
            values = lags_of(state[chunk], moved[chunk], receivers, table, base, some, first, hours, last)
            last = mine[at, kind] = values[0]
            cross[at] = values[-1]
            if kind != "i" and at < 3:
                inward[at, kind] = over_hour(last, INWARD)
        elif kind == "k":
            last = mine[at, kind] = lags_of_rest(cross[at], table, last)
            inward[at, kind] = over_hour(last, INWARD)
        elif kind in "mn":
            which, low = ("l", 0) if kind == "m" else ("k", SPLITS[at])
            part = (0, mine[0, "i"]) if at == 0 else (low, mine[at, which])
            high = low + inward[at, which].shape[0]
            last = sum_of([part, (low, inward[at, which])], low, high, jnp.bfloat16, last)
            middle[at, which] = over_hour(last, MIDDLE)
        elif kind in "fg":
            which, part = ("l", 0) if kind == "f" else ("k", 1)
            parts = [(0, mine[2, "l"]), (cuts[part], middle[0, which])]
            last = sum_of(parts, cuts[part], cuts[part + 1], jnp.bfloat16, last)
            outward[which] = over_hour(last, OUTWARD)
        elif kind == "h":
            parts = [(0, mine[3, "l"]), (0, outward["l"]), (0, middle[1, "l"])]
            early = last = sum_of(parts, 0, cuts[1], jnp.float32, last)
        elif kind == "p":
            parts = [(0, early), (cuts[1], mine[3, "l"][cuts[1] :]), (cuts[1], outward["k"])]
            parts += [(SPLITS[1], middle[1, "k"])]
            last = sum_of(parts, 0, 8, jnp.float32, last)
    return sum_of([(0, last), (0, inward[2, "l"])], 0, 8, jnp.bfloat16, last, final=True)


def solution(mesh):
    placed = (P(None, "hour", None, "chan"), P("hour", "chan"), P())
    return jax.shard_map(
        functools.partial(body, mesh.shape["chan"]),
        mesh=mesh,
        in_specs=placed,
        out_specs=P("hour", None, "chan"),
        check_vma=False,
    )
```

```python
import functools
import math

import jax
import jax.numpy as jnp
from jax import lax
from jax.experimental import pallas as pl
from jax.experimental.pallas import tpu as pltpu
from jax.sharding import PartitionSpec as P

LAGS = 512
GROUP = 16
ORDER = ((3, 2, 1, 0), (3, 2, 0, 1), (0, 1, 3, 2), (0, 1, 2, 3))
SPLITS = (4, 2, 8, 8)
STEPS = (
    "r0", "q", "r0", "w", "t", "r0", "r1", "r2", "l0", "r1", "k0",
    "i0", "r1", "r2", "l1", "m0", "r2", "k1", "n0", "l2", "m1", "f", "l3", "g", "h", "n1", "p",
)
INWARD = ((0, 1), (3, 2))
MIDDLE = ((1, 2), (2, 1))
OUTWARD = ((1, 0), (2, 3))
ENDS, INNER = (0, 3), (1, 2)
MIB = 1024 * 1024
COST = pl.CostEstimate(flops=1, bytes_accessed=1, transcendentals=0)

HBM = pl.BlockSpec(memory_space=pltpu.HBM)
ANY = pl.BlockSpec(memory_space=pl.ANY)
VMEM = pl.BlockSpec(memory_space=pltpu.VMEM)


def quarter_of(hour, slot):
    quarter = jnp.int32(ORDER[0][slot])
    for row in range(1, 4):
        quarter = jnp.where(hour == row, jnp.int32(ORDER[row][slot]), quarter)
    return quarter


def shares(window_count, freq_count):
    middle = freq_count // (2 * GROUP) * 2 // 3 * 2 * GROUP
    half = window_count // 2
    return [
        ((low, low + half), bins) for low in (0, half) for bins in ((0, middle), (middle, freq_count))
    ]


def pick_share(data_ref, onehot, usable, windows, bins, own_refs, other_refs, total=None):
    channels_here = data_ref.shape[3]
    narrow = usable.shape[1] // 2
    per_slot = onehot.shape[0] // len(own_refs)
    lanes = slice(windows[0] * GROUP, windows[1] * GROUP)
    usable_here = jnp.concatenate([usable[:, lanes]] * 2, 1)
    even = (lax.axis_index("chan") % 2) == 0
    for pair in range(bins[0] // (2 * GROUP), bins[1] // (2 * GROUP)):
        picked = []
        for part in range(2):
            both = []
            for group in (2 * pair, 2 * pair + 1):
                columns = data_ref[part, windows[0] : windows[1], group * GROUP : (group + 1) * GROUP, :]
                if total is not None:
                    value = columns.astype(jnp.float32)
                    square = value * value
                    total = total + (square[:, :8] + square[:, 8:])
                both.append(columns.reshape(narrow, channels_here))
            picked.append(
                lax.dot_general(
                    onehot,
                    jnp.concatenate(both, 0),
                    (((1,), (1,)), ((), ())),
                    preferred_element_type=jnp.float32,
                )
                * usable_here
            )
        for refs, value in (
            (own_refs, jnp.where(even, picked[0], picked[1])),
            (other_refs, jnp.where(even, picked[1], picked[0])),
        ):
            for at, (ref, base) in enumerate(refs):
                rows = slice(at * per_slot, (at + 1) * per_slot)
                both = jnp.concatenate([value[rows, :narrow], value[rows, narrow:]], 0)
                ref[base + pair * 16 : base + pair * 16 + 16, lanes] = both.astype(jnp.bfloat16)
    return total


def front_kernel(
    sources_hbm, spectra_hbm, quality_hbm,
    own_ref, other_ref, data_ref, onehot_ref, usable_ref, quality_ref,
    sources_ref, flags_ref, sems, small_sems,
):
    small = [
        pltpu.make_async_copy(sources_hbm, sources_ref, small_sems.at[0]),
        pltpu.make_async_copy(quality_hbm, flags_ref, small_sems.at[1]),
    ]
    _, window_count, freq_count, channels_here = data_ref.shape
    large = []
    for at, (windows, bins) in enumerate(shares(window_count, freq_count)):
        part = (slice(None), pl.ds(windows[0], windows[1] - windows[0]), pl.ds(bins[0], bins[1] - bins[0]))
        large.append(pltpu.make_async_copy(spectra_hbm.at[part], data_ref.at[part], sems.at[at]))
    for copy in small + large:
        copy.start()
    source_count = sources_ref.shape[0]
    per_slot = source_count // 4
    wide = window_count * GROUP
    chan = lax.axis_index("chan")
    hour = lax.axis_index("hour")
    for copy in small:
        copy.wait()
    row = lax.broadcasted_iota(jnp.int32, (source_count, channels_here), 0)
    lane = lax.broadcasted_iota(jnp.int32, (source_count, channels_here), 1)
    wanted = jnp.full((source_count, channels_here), -1, jnp.int32)
    for slot in range(4):
        first = quarter_of(hour, slot) * per_slot
        for at in range(per_slot):
            wanted = jnp.where(row == slot * per_slot + at, sources_ref[first + at], wanted)
    onehot = (wanted - chan * channels_here == lane).astype(jnp.float32)
    quality = flags_ref[...].astype(jnp.float32)
    usable = lax.dot_general(
        onehot.astype(jnp.bfloat16),
        quality.astype(jnp.bfloat16),
        (((1,), (1,)), ((), ())),
        preferred_element_type=jnp.float32,
    )
    spread = (
        lax.broadcasted_iota(jnp.int32, (window_count, wide), 1) // GROUP
        == lax.broadcasted_iota(jnp.int32, (window_count, wide), 0)
    )
    usable = jnp.dot(
        usable.astype(jnp.bfloat16),
        spread.astype(jnp.float32).astype(jnp.bfloat16),
        preferred_element_type=jnp.float32,
    )
    onehot_ref[...] = onehot
    usable_ref[...] = usable
    quality_ref[...] = quality
    onehot = onehot[:per_slot].astype(jnp.bfloat16)
    for copy, (windows, bins) in zip(large, shares(window_count, freq_count)):
        copy.wait()
        pick_share(data_ref, onehot, usable[:per_slot], windows, bins, [(own_ref, 0)], [(other_ref, 0)])


def front(spectra, quality, sources):
    _, window_count, freq_count, channels_here = spectra.shape
    rows = freq_count // GROUP * sources.shape[0] // 4
    wide = window_count * GROUP
    steps = len(shares(window_count, freq_count))
    return pl.pallas_call(
        front_kernel,
        in_specs=[HBM, HBM, HBM],
        out_specs=[VMEM] * 6,
        out_shape=[
            jax.ShapeDtypeStruct((rows, wide), jnp.bfloat16),
            jax.ShapeDtypeStruct((rows, wide), jnp.bfloat16),
            jax.ShapeDtypeStruct(spectra.shape, jnp.bfloat16),
            jax.ShapeDtypeStruct((sources.shape[0], channels_here), jnp.float32),
            jax.ShapeDtypeStruct((sources.shape[0], wide), jnp.float32),
            jax.ShapeDtypeStruct(quality.shape, jnp.float32),
        ],
        scratch_shapes=[
            pltpu.SMEM(sources.shape, jnp.int32),
            pltpu.VMEM(quality.shape, jnp.int32),
            pltpu.SemaphoreType.DMA((steps,)),
            pltpu.SemaphoreType.DMA((2,)),
        ],
        compiler_params=pltpu.CompilerParams(vmem_limit_bytes=16 * MIB),
        cost_estimate=COST,
        name="pick_first",
    )(*(pltpu.with_memory_space_constraint(value, pltpu.HBM) for value in (sources, spectra, quality)))


def rest_kernel(
    data_ref, onehot_ref, usable_ref, quality_ref, after_ref,
    own_second_ref, own_rest_ref, other_second_ref, other_rest_ref, scale_ref,
):
    _, window_count, freq_count, channels_here = data_ref.shape
    rows = own_second_ref.shape[0]
    per_slot = onehot_ref.shape[0] // 4
    onehot = onehot_ref[per_slot:, :].astype(jnp.bfloat16)
    usable = usable_ref[per_slot:, :]
    own_refs = [(own_second_ref, 0), (own_rest_ref, 0), (own_rest_ref, rows)]
    other_refs = [(other_second_ref, 0), (other_rest_ref, 0), (other_rest_ref, rows)]
    totals = {}
    for windows, bins in shares(window_count, freq_count):
        total = totals.get(windows, jnp.zeros((windows[1] - windows[0], 8, channels_here), jnp.float32))
        totals[windows] = pick_share(data_ref, onehot, usable, windows, bins, own_refs, other_refs, total)
    power = jnp.concatenate([jnp.sum(total, axis=1) for total in totals.values()], 0) / freq_count
    scale_ref[...] = lax.rsqrt(power + 1e-06) * quality_ref[...]


def pick_rest(data, onehot, usable, quality, rows, after):
    shape = lambda slots: jax.ShapeDtypeStruct((slots * rows, usable.shape[1]), jnp.bfloat16)
    return pl.pallas_call(
        rest_kernel,
        in_specs=[VMEM] * 4 + [ANY],
        out_specs=[VMEM] * 5,
        out_shape=[shape(1), shape(2), shape(1), shape(2), jax.ShapeDtypeStruct(quality.shape, jnp.float32)],
        compiler_params=pltpu.CompilerParams(vmem_limit_bytes=16 * MIB),
        cost_estimate=COST,
        name="pick_rest",
    )(data, onehot, usable, quality, after)


def whiten_kernel(data_ref, scale_ref, after_ref, out_ref):
    _, window_count, freq_count, _ = data_ref.shape
    step = freq_count // 5
    for window in range(window_count):
        scale = scale_ref[window : window + 1, :]

        def apply(i, carry):
            bins = pl.ds(pl.multiple_of(i * step, step), step)
            for part in range(2):
                value = data_ref[part, window, bins, :].astype(jnp.float32) * scale
                out_ref[part, window, bins, :] = value.astype(jnp.bfloat16)
            return carry

        lax.fori_loop(0, freq_count // step, apply, 0)


def whiten(data, scale, after):
    return pl.pallas_call(
        whiten_kernel,
        in_specs=[VMEM, VMEM, ANY],
        out_specs=VMEM,
        out_shape=jax.ShapeDtypeStruct(data.shape, jnp.bfloat16),
        compiler_params=pltpu.CompilerParams(vmem_limit_bytes=16 * MIB),
        cost_estimate=COST,
        name="whiten_receivers",
    )(data, scale, after)


def add_kernel(count, *refs):
    total = refs[0][...].astype(jnp.float32)
    for ref in refs[1:count]:
        total = total + ref[...].astype(jnp.float32)
    refs[-1][...] = total.astype(refs[-1].dtype)


def add_after(after, *values):
    return pl.pallas_call(
        functools.partial(add_kernel, len(values)),
        in_specs=[VMEM] * len(values) + [ANY],
        out_specs=VMEM,
        out_shape=jax.ShapeDtypeStruct(values[0].shape, values[0].dtype),
        compiler_params=pltpu.CompilerParams(vmem_limit_bytes=16 * MIB),
        cost_estimate=COST,
        name="add",
    )(*values, after)


def table_kernel(after_ref, out_ref):
    lag_count, columns = out_ref.shape
    freq_count = columns // 2
    highs = lag_count // GROUP

    def angle(count, lag_of, offset):
        lag = lag_of(lax.broadcasted_iota(jnp.int32, (count, columns), 0)).astype(jnp.float32)
        column = lax.broadcasted_iota(jnp.int32, (count, columns), 1).astype(jnp.float32)
        part = (column >= freq_count).astype(jnp.float32)
        turns = (column - part * freq_count + 1.0) * lag + part * offset
        turns = turns - columns * jnp.round(turns * (1.0 / columns))
        return turns * (math.pi / freq_count)

    high = angle(highs, lambda row: row * GROUP - lag_count // 2, freq_count // 2)
    low = angle(GROUP, lambda row: row, 0)
    cos_high, sin_high = jnp.cos(high), jnp.sin(high)
    cos_low, sin_low = jnp.cos(low) / freq_count, jnp.sin(low) / freq_count
    for row in range(highs):
        value = cos_high[row : row + 1] * cos_low - sin_high[row : row + 1] * sin_low
        out_ref[row * GROUP : (row + 1) * GROUP, :] = value.astype(jnp.bfloat16)


def lag_table(freq_count, lag_count, after):
    return pl.pallas_call(
        table_kernel,
        in_specs=[ANY],
        out_specs=VMEM,
        out_shape=jax.ShapeDtypeStruct((lag_count, 2 * freq_count), jnp.bfloat16),
        compiler_params=pltpu.CompilerParams(vmem_limit_bytes=16 * MIB),
        cost_estimate=COST,
        name="lag_table",
    )(after)


def lags_kernel(base, sources, done, hours, *refs):
    hour = lax.axis_index("hour")
    here = functools.reduce(jnp.logical_or, [hour == value for value in hours])

    @pl.when(here)
    def _():
        make_lags(base, sources, done, *refs)


def make_lags(base, sources, done, own_ref, other_ref, receivers_ref, table_ref, after_ref, out_ref, *refs):
    spec_ref, cross_ref = refs[-2:]
    count = len(sources)
    _, window_count, freq_count, channels_here = receivers_ref.shape
    wide = own_ref.shape[1]
    groups = freq_count // GROUP
    even = (lax.axis_index("chan") % 2) == 0

    def load(i):
        rows = pl.ds(pl.multiple_of(base + i * 16, 16), 16)
        own = own_ref[rows, :].astype(jnp.float32)
        other = other_ref[rows, :].astype(jnp.float32)
        return jnp.where(even, own, other), jnp.where(even, other, own)

    def add(i, total):
        real, imag = load(i)
        square = real * real + imag * imag
        return total + square[:8] + square[8:]

    total = lax.fori_loop(0, groups // 2, add, jnp.zeros((8, wide), jnp.float32), unroll=groups // 2)
    same = (
        lax.broadcasted_iota(jnp.int32, (wide, wide), 0) // GROUP
        == lax.broadcasted_iota(jnp.int32, (wide, wide), 1) // GROUP
    ).astype(jnp.float32)
    power = jnp.dot(total, same, preferred_element_type=jnp.float32, precision=lax.Precision.HIGHEST)
    scale = lax.rsqrt(power / freq_count + 1e-06)
    scale = jnp.concatenate([scale, scale], 0)

    def apply(i, carry):
        rows = pl.ds(pl.multiple_of(i * 16, 16), 16)
        for part, value in enumerate(load(i)):
            spec_ref[part, rows, :] = (value * scale).astype(jnp.bfloat16).astype(jnp.float32)
        return carry

    lax.fori_loop(0, groups // 2, apply, 0, unroll=groups // 2)

    diagonal = [
        lax.broadcasted_iota(jnp.int32, (8, wide), 1) % GROUP
        == lax.broadcasted_iota(jnp.int32, (8, wide), 0) + low
        for low in (0, 8)
    ]
    zero = jnp.zeros((8, wide), jnp.float32)

    def cross_of(group, carry):
        tiles = []
        for part in range(2):
            rows = spec_ref[part, pl.ds(pl.multiple_of(group * 8, 8), 8), :]
            for at in sources:
                row = jnp.broadcast_to(rows[at : at + 1, :], (8, wide))
                tiles += [jnp.where(mask, row, zero) for mask in diagonal]
        bins = pl.ds(pl.multiple_of(group * GROUP, GROUP), GROUP)
        real = receivers_ref[0, :, bins, :].reshape(wide, channels_here)
        imag = receivers_ref[1, :, bins, :].reshape(wide, channels_here)
        cross = jnp.dot(
            jnp.concatenate(tiles, 0).astype(jnp.bfloat16),
            jnp.concatenate([real, imag], 1),
            preferred_element_type=jnp.float32,
        )
        half = count * GROUP
        parts = (
            cross[:half, :channels_here] + cross[half:, channels_here:],
            cross[:half, channels_here:] - cross[half:, :channels_here],
        )
        for part, value in enumerate(parts):
            value = value.astype(jnp.bfloat16)
            rows = pl.ds(pl.multiple_of(part * freq_count + group * GROUP, GROUP), GROUP)
            for at in range(count):
                ref, pair = (cross_ref, at // 2) if at < done else (refs[0], (at - done) // 2)
                lanes = slice((at % 2) * channels_here, (at % 2 + 1) * channels_here)
                ref[pair, rows, lanes] = value[at * GROUP : (at + 1) * GROUP]
        return carry

    lax.fori_loop(0, groups, cross_of, 0, unroll=groups)
    transform(cross_ref, table_ref, out_ref)


def transform(cross_ref, table_ref, out_ref):
    channels_here = out_ref.shape[2]
    rows = 128
    for pair in range(cross_ref.shape[0]):
        for block in range(table_ref.shape[0] // rows):
            lags = slice(block * rows, (block + 1) * rows)
            value = jnp.dot(
                table_ref[lags, :], cross_ref[pair], preferred_element_type=jnp.float32
            ).astype(jnp.bfloat16)
            out_ref[2 * pair, lags, :] = value[:, :channels_here]
            out_ref[2 * pair + 1, lags, :] = value[:, channels_here:]


def lags_of(own, other, receivers, table, base, sources, done, hours, after):
    _, window_count, freq_count, channels_here = receivers.shape
    wide = own.shape[1]
    count = len(sources)
    cross = lambda some: (some // 2, 2 * freq_count, 2 * channels_here)
    out_shape = [jax.ShapeDtypeStruct((done, table.shape[0], channels_here), jnp.bfloat16)]
    if done < count:
        out_shape.append(jax.ShapeDtypeStruct(cross(count - done), jnp.bfloat16))
    return pl.pallas_call(
        functools.partial(lags_kernel, base, sources, done, hours),
        in_specs=[VMEM] * 4 + [ANY],
        out_specs=[VMEM] * len(out_shape),
        out_shape=out_shape,
        scratch_shapes=[
            pltpu.VMEM((2, freq_count // GROUP * 8, wide), jnp.float32),
            pltpu.VMEM(cross(done), jnp.bfloat16),
        ],
        compiler_params=pltpu.CompilerParams(vmem_limit_bytes=16 * MIB),
        cost_estimate=COST,
        name="lags",
    )(own, other, receivers, table, after)


def lags_of_rest(cross, table, after):
    pairs, _, lanes = cross.shape
    return pl.pallas_call(
        lambda cross_ref, table_ref, after_ref, out_ref: transform(cross_ref, table_ref, out_ref),
        in_specs=[VMEM, VMEM, ANY],
        out_specs=VMEM,
        out_shape=jax.ShapeDtypeStruct((2 * pairs, table.shape[0], lanes // 2), jnp.bfloat16),
        compiler_params=pltpu.CompilerParams(vmem_limit_bytes=16 * MIB),
        cost_estimate=COST,
        name="lags_rest",
    )(cross, table, after)


def sum_kernel(firsts, low, *refs):
    out_ref, rest = refs[len(firsts) + 1], refs[len(firsts) + 2 :]
    total_ref = rest[0] if rest else out_ref
    copies = []
    for source in range(low, low + out_ref.shape[0]):
        total = 0.0
        for first, ref in zip(firsts, refs):
            if first <= source < first + ref.shape[0]:
                total = total + ref[source - first].astype(jnp.float32)
        total_ref[source - low] = total.astype(total_ref.dtype)
        if rest and source % 2:
            pair = pl.ds(source - 1, 2)
            copies.append(
                pltpu.make_async_copy(total_ref.at[pair], out_ref.at[pair], rest[1].at[source // 2])
            )
            copies[-1].start()
    for copy in copies:
        copy.wait()


def sum_of(parts, low, high, dtype, after, final=False):
    firsts, values = zip(*parts)
    shape = (high - low,) + values[0].shape[1:]
    scratch = [pltpu.VMEM(shape, dtype), pltpu.SemaphoreType.DMA(((high - low) // 2,))]
    return pl.pallas_call(
        functools.partial(sum_kernel, firsts, low),
        in_specs=[VMEM] * len(values) + [ANY],
        out_specs=HBM if final else VMEM,
        out_shape=jax.ShapeDtypeStruct(shape, dtype),
        scratch_shapes=scratch if final else [],
        compiler_params=pltpu.CompilerParams(vmem_limit_bytes=16 * MIB),
        cost_estimate=COST,
        name="sum",
    )(*values, after)


def chip_stages(chan_count):
    bits = [1 << b for b in range(1, chan_count.bit_length() - 1)]
    turned = bits[1:] + bits[:1]
    return [
        [(i, i ^ (odd_bit if i % 2 else even_bit)) for i in range(chan_count)]
        for even_bit, odd_bit in zip(bits, turned)
    ]


def body(chan_count, spectra, quality, sources):
    freq_count = spectra.shape[2]
    stages = chip_stages(chan_count)
    cores = [(i, i ^ 1) for i in range(chan_count)]
    over_chan = lambda value, pairs: lax.ppermute(value, "chan", pairs)
    over_hour = lambda value, pairs: lax.ppermute(value, "hour", pairs)

    own, other, data, onehot, usable, flags = front(spectra, quality, sources)
    slot_rows = own.shape[0]
    state = {0: own}
    moved = {0: over_chan(other, cores)}
    passes = [0, 0, 0]
    made, mine, cross, middle, outward = {}, {}, {}, {}, {}
    inward = {}
    cuts = (0, SPLITS[0], 8)
    last = onehot
    for step in STEPS:
        kind, at = step[0], int(step[1:] or 0)
        if kind == "r":
            for pairs in (stages[:1], stages[1:], [cores])[passes[at]]:
                last = state[at] = add_after(last, state[at], moved[at])
                moved[at] = over_chan(last, pairs)
            passes[at] += 1
        elif kind == "q":
            state[1], state[2], *others, scale = pick_rest(data, onehot, usable, flags, slot_rows, last)
            moved.update({1 + chunk: over_chan(value, cores) for chunk, value in enumerate(others)})
            last = scale
        elif kind == "t":
            table = last = lag_table(freq_count, LAGS, last)
        elif kind == "w":
            receivers = last = whiten(data, scale, last)
        elif kind in "li" or step == "k0":
            chunk = min(at, 2)
            some, first, hours = range(8), SPLITS[at], (0, 1, 2, 3)
            if at == 0:
                some = {"l": range(first), "k": range(first, 8), "i": range(8)}[kind]
                first, hours = len(some), INNER if kind == "i" else ENDS
            base = slot_rows * (at - chunk)
            values = lags_of(state[chunk], moved[chunk], receivers, table, base, some, first, hours, last)
            last = mine[at, kind] = values[0]
            cross[at] = values[-1]
            if kind != "i" and at < 3:
                inward[at, kind] = over_hour(last, INWARD)
        elif kind == "k":
            last = mine[at, kind] = lags_of_rest(cross[at], table, last)
            inward[at, kind] = over_hour(last, INWARD)
        elif kind in "mn":
            which, low = ("l", 0) if kind == "m" else ("k", SPLITS[at])
            part = (0, mine[0, "i"]) if at == 0 else (low, mine[at, which])
            high = low + inward[at, which].shape[0]
            last = sum_of([part, (low, inward[at, which])], low, high, jnp.bfloat16, last)
            middle[at, which] = over_hour(last, MIDDLE)
        elif kind in "fg":
            which, part = ("l", 0) if kind == "f" else ("k", 1)
            parts = [(0, mine[2, "l"]), (cuts[part], middle[0, which])]
            last = sum_of(parts, cuts[part], cuts[part + 1], jnp.bfloat16, last)
            outward[which] = over_hour(last, OUTWARD)
        elif kind == "h":
            parts = [(0, mine[3, "l"]), (0, outward["l"]), (0, middle[1, "l"])]
            early = last = sum_of(parts, 0, cuts[1], jnp.float32, last)
        elif kind == "p":
            parts = [(0, early), (cuts[1], mine[3, "l"][cuts[1] :]), (cuts[1], outward["k"])]
            parts += [(SPLITS[1], middle[1, "k"])]
            last = sum_of(parts, 0, 8, jnp.float32, last)
    return sum_of([(0, last), (0, inward[2, "l"])], 0, 8, jnp.bfloat16, last, final=True)


def solution(mesh):
    placed = (P(None, "hour", None, "chan"), P("hour", "chan"), P())
    return jax.shard_map(
        functools.partial(body, mesh.shape["chan"]),
        mesh=mesh,
        in_specs=placed,
        out_specs=P("hour", None, "chan"),
        check_vma=False,
    )
```

```python
import functools
import math

import jax
import jax.numpy as jnp
from jax import lax
from jax.experimental import pallas as pl
from jax.experimental.pallas import tpu as pltpu
from jax.sharding import PartitionSpec as P

LAGS = 512
GROUP = 16
ORDER = ((3, 2, 1, 0), (3, 2, 0, 1), (0, 1, 3, 2), (0, 1, 2, 3))
SPLITS = (4, 2, 8, 8)
STEPS = (
    "r0", "q", "r0", "w", "t", "r0", "r1", "r2", "l0", "r1", "k0",
    "i0", "r1", "r2", "l1", "m0", "r2", "k1", "n0", "l2", "m1", "f", "l3", "g", "h", "n1", "p",
)
INWARD = ((0, 1), (3, 2))
MIDDLE = ((1, 2), (2, 1))
OUTWARD = ((1, 0), (2, 3))
ENDS, INNER = (0, 3), (1, 2)
MIB = 1024 * 1024
COST = pl.CostEstimate(flops=1, bytes_accessed=1, transcendentals=0)

HBM = pl.BlockSpec(memory_space=pltpu.HBM)
ANY = pl.BlockSpec(memory_space=pl.ANY)
VMEM = pl.BlockSpec(memory_space=pltpu.VMEM)


def quarter_of(hour, slot):
    quarter = jnp.int32(ORDER[0][slot])
    for row in range(1, 4):
        quarter = jnp.where(hour == row, jnp.int32(ORDER[row][slot]), quarter)
    return quarter


def shares(window_count, freq_count):
    middle = freq_count // (2 * GROUP) * 2 // 3 * 2 * GROUP
    half = window_count // 2
    return [
        ((low, low + half), bins) for low in (0, half) for bins in ((0, middle), (middle, freq_count))
    ]


def pick_share(data_ref, onehot, usable, windows, bins, own_refs, other_refs, total=None):
    channels_here = data_ref.shape[3]
    narrow = usable.shape[1] // 2
    per_slot = onehot.shape[0] // len(own_refs)
    lanes = slice(windows[0] * GROUP, windows[1] * GROUP)
    usable_here = jnp.concatenate([usable[:, lanes]] * 2, 1)
    even = (lax.axis_index("chan") % 2) == 0
    for pair in range(bins[0] // (2 * GROUP), bins[1] // (2 * GROUP)):
        picked = []
        for part in range(2):
            both = []
            for group in (2 * pair, 2 * pair + 1):
                columns = data_ref[part, windows[0] : windows[1], group * GROUP : (group + 1) * GROUP, :]
                if total is not None:
                    value = columns.astype(jnp.float32)
                    square = value * value
                    total = total + (square[:, :8] + square[:, 8:])
                both.append(columns.reshape(narrow, channels_here))
            picked.append(
                lax.dot_general(
                    onehot,
                    jnp.concatenate(both, 0),
                    (((1,), (1,)), ((), ())),
                    preferred_element_type=jnp.float32,
                )
                * usable_here
            )
        for refs, value in (
            (own_refs, jnp.where(even, picked[0], picked[1])),
            (other_refs, jnp.where(even, picked[1], picked[0])),
        ):
            for at, (ref, base) in enumerate(refs):
                rows = slice(at * per_slot, (at + 1) * per_slot)
                both = jnp.concatenate([value[rows, :narrow], value[rows, narrow:]], 0)
                ref[base + pair * 16 : base + pair * 16 + 16, lanes] = both.astype(jnp.bfloat16)
    return total


def front_kernel(
    sources_hbm, spectra_hbm, quality_hbm,
    own_ref, other_ref, data_ref, onehot_ref, usable_ref, quality_ref,
    sources_ref, flags_ref, sems, small_sems,
):
    small = [
        pltpu.make_async_copy(sources_hbm, sources_ref, small_sems.at[0]),
        pltpu.make_async_copy(quality_hbm, flags_ref, small_sems.at[1]),
    ]
    _, window_count, freq_count, channels_here = data_ref.shape
    large = []
    for at, (windows, bins) in enumerate(shares(window_count, freq_count)):
        part = (slice(None), pl.ds(windows[0], windows[1] - windows[0]), pl.ds(bins[0], bins[1] - bins[0]))
        large.append(pltpu.make_async_copy(spectra_hbm.at[part], data_ref.at[part], sems.at[at]))
    for copy in small + large:
        copy.start()
    source_count = sources_ref.shape[0]
    per_slot = source_count // 4
    wide = window_count * GROUP
    chan = lax.axis_index("chan")
    hour = lax.axis_index("hour")
    for copy in small:
        copy.wait()
    row = lax.broadcasted_iota(jnp.int32, (source_count, channels_here), 0)
    lane = lax.broadcasted_iota(jnp.int32, (source_count, channels_here), 1)
    wanted = jnp.full((source_count, channels_here), -1, jnp.int32)
    for slot in range(4):
        first = quarter_of(hour, slot) * per_slot
        for at in range(per_slot):
            wanted = jnp.where(row == slot * per_slot + at, sources_ref[first + at], wanted)
    onehot = (wanted - chan * channels_here == lane).astype(jnp.float32)
    quality = flags_ref[...].astype(jnp.float32)
    usable = lax.dot_general(
        onehot.astype(jnp.bfloat16),
        quality.astype(jnp.bfloat16),
        (((1,), (1,)), ((), ())),
        preferred_element_type=jnp.float32,
    )
    spread = (
        lax.broadcasted_iota(jnp.int32, (window_count, wide), 1) // GROUP
        == lax.broadcasted_iota(jnp.int32, (window_count, wide), 0)
    )
    usable = jnp.dot(
        usable.astype(jnp.bfloat16),
        spread.astype(jnp.float32).astype(jnp.bfloat16),
        preferred_element_type=jnp.float32,
    )
    onehot_ref[...] = onehot
    usable_ref[...] = usable
    quality_ref[...] = quality
    onehot = onehot[:per_slot].astype(jnp.bfloat16)
    for copy, (windows, bins) in zip(large, shares(window_count, freq_count)):
        copy.wait()
        pick_share(data_ref, onehot, usable[:per_slot], windows, bins, [(own_ref, 0)], [(other_ref, 0)])


def front(spectra, quality, sources):
    _, window_count, freq_count, channels_here = spectra.shape
    rows = freq_count // GROUP * sources.shape[0] // 4
    wide = window_count * GROUP
    steps = len(shares(window_count, freq_count))
    return pl.pallas_call(
        front_kernel,
        in_specs=[HBM, HBM, HBM],
        out_specs=[VMEM] * 6,
        out_shape=[
            jax.ShapeDtypeStruct((rows, wide), jnp.bfloat16),
            jax.ShapeDtypeStruct((rows, wide), jnp.bfloat16),
            jax.ShapeDtypeStruct(spectra.shape, jnp.bfloat16),
            jax.ShapeDtypeStruct((sources.shape[0], channels_here), jnp.float32),
            jax.ShapeDtypeStruct((sources.shape[0], wide), jnp.float32),
            jax.ShapeDtypeStruct(quality.shape, jnp.float32),
        ],
        scratch_shapes=[
            pltpu.SMEM(sources.shape, jnp.int32),
            pltpu.VMEM(quality.shape, jnp.int32),
            pltpu.SemaphoreType.DMA((steps,)),
            pltpu.SemaphoreType.DMA((2,)),
        ],
        compiler_params=pltpu.CompilerParams(vmem_limit_bytes=16 * MIB),
        cost_estimate=COST,
        name="pick_first",
    )(*(pltpu.with_memory_space_constraint(value, pltpu.HBM) for value in (sources, spectra, quality)))


def rest_kernel(
    data_ref, onehot_ref, usable_ref, quality_ref, after_ref,
    own_second_ref, own_rest_ref, other_second_ref, other_rest_ref, scale_ref,
):
    _, window_count, freq_count, channels_here = data_ref.shape
    rows = own_second_ref.shape[0]
    per_slot = onehot_ref.shape[0] // 4
    onehot = onehot_ref[per_slot:, :].astype(jnp.bfloat16)
    usable = usable_ref[per_slot:, :]
    own_refs = [(own_second_ref, 0), (own_rest_ref, 0), (own_rest_ref, rows)]
    other_refs = [(other_second_ref, 0), (other_rest_ref, 0), (other_rest_ref, rows)]
    totals = {}
    for windows, bins in shares(window_count, freq_count):
        total = totals.get(windows, jnp.zeros((windows[1] - windows[0], 8, channels_here), jnp.float32))
        totals[windows] = pick_share(data_ref, onehot, usable, windows, bins, own_refs, other_refs, total)
    power = jnp.concatenate([jnp.sum(total, axis=1) for total in totals.values()], 0) / freq_count
    scale_ref[...] = lax.rsqrt(power + 1e-06) * quality_ref[...]


def pick_rest(data, onehot, usable, quality, rows, after):
    shape = lambda slots: jax.ShapeDtypeStruct((slots * rows, usable.shape[1]), jnp.bfloat16)
    return pl.pallas_call(
        rest_kernel,
        in_specs=[VMEM] * 4 + [ANY],
        out_specs=[VMEM] * 5,
        out_shape=[shape(1), shape(2), shape(1), shape(2), jax.ShapeDtypeStruct(quality.shape, jnp.float32)],
        compiler_params=pltpu.CompilerParams(vmem_limit_bytes=16 * MIB),
        cost_estimate=COST,
        name="pick_rest",
    )(data, onehot, usable, quality, after)


def whiten_kernel(data_ref, scale_ref, after_ref, out_ref):
    _, window_count, freq_count, _ = data_ref.shape
    step = freq_count // 5
    for window in range(window_count):
        scale = scale_ref[window : window + 1, :]

        def apply(i, carry):
            bins = pl.ds(pl.multiple_of(i * step, step), step)
            for part in range(2):
                value = data_ref[part, window, bins, :].astype(jnp.float32) * scale
                out_ref[part, window, bins, :] = value.astype(jnp.bfloat16)
            return carry

        lax.fori_loop(0, freq_count // step, apply, 0)


def whiten(data, scale, after):
    return pl.pallas_call(
        whiten_kernel,
        in_specs=[VMEM, VMEM, ANY],
        out_specs=VMEM,
        out_shape=jax.ShapeDtypeStruct(data.shape, jnp.bfloat16),
        compiler_params=pltpu.CompilerParams(vmem_limit_bytes=16 * MIB),
        cost_estimate=COST,
        name="whiten_receivers",
    )(data, scale, after)


def add_kernel(count, *refs):
    total = refs[0][...].astype(jnp.float32)
    for ref in refs[1:count]:
        total = total + ref[...].astype(jnp.float32)
    refs[-1][...] = total.astype(refs[-1].dtype)


def add_after(after, *values):
    return pl.pallas_call(
        functools.partial(add_kernel, len(values)),
        in_specs=[VMEM] * len(values) + [ANY],
        out_specs=VMEM,
        out_shape=jax.ShapeDtypeStruct(values[0].shape, values[0].dtype),
        compiler_params=pltpu.CompilerParams(vmem_limit_bytes=16 * MIB),
        cost_estimate=COST,
        name="add",
    )(*values, after)


def table_kernel(after_ref, out_ref):
    lag_count, columns = out_ref.shape
    freq_count = columns // 2
    highs = lag_count // GROUP

    def angle(count, lag_of, offset):
        lag = lag_of(lax.broadcasted_iota(jnp.int32, (count, columns), 0)).astype(jnp.float32)
        column = lax.broadcasted_iota(jnp.int32, (count, columns), 1).astype(jnp.float32)
        part = (column >= freq_count).astype(jnp.float32)
        turns = (column - part * freq_count + 1.0) * lag + part * offset
        turns = turns - columns * jnp.round(turns * (1.0 / columns))
        return turns * (math.pi / freq_count)

    high = angle(highs, lambda row: row * GROUP - lag_count // 2, freq_count // 2)
    low = angle(GROUP, lambda row: row, 0)
    cos_high, sin_high = jnp.cos(high), jnp.sin(high)
    cos_low, sin_low = jnp.cos(low) / freq_count, jnp.sin(low) / freq_count
    for row in range(highs):
        value = cos_high[row : row + 1] * cos_low - sin_high[row : row + 1] * sin_low
        out_ref[row * GROUP : (row + 1) * GROUP, :] = value.astype(jnp.bfloat16)


def lag_table(freq_count, lag_count, after):
    return pl.pallas_call(
        table_kernel,
        in_specs=[ANY],
        out_specs=VMEM,
        out_shape=jax.ShapeDtypeStruct((lag_count, 2 * freq_count), jnp.bfloat16),
        compiler_params=pltpu.CompilerParams(vmem_limit_bytes=16 * MIB),
        cost_estimate=COST,
        name="lag_table",
    )(after)


def lags_kernel(base, sources, done, hours, *refs):
    hour = lax.axis_index("hour")
    here = functools.reduce(jnp.logical_or, [hour == value for value in hours])

    @pl.when(here)
    def _():
        make_lags(base, sources, done, *refs)


def make_lags(base, sources, done, own_ref, other_ref, receivers_ref, table_ref, after_ref, out_ref, *refs):
    spec_ref, cross_ref = refs[-2:]
    count = len(sources)
    _, window_count, freq_count, channels_here = receivers_ref.shape
    wide = own_ref.shape[1]
    groups = freq_count // GROUP
    even = (lax.axis_index("chan") % 2) == 0

    def load(i):
        rows = pl.ds(pl.multiple_of(base + i * 16, 16), 16)
        own = own_ref[rows, :].astype(jnp.float32)
        other = other_ref[rows, :].astype(jnp.float32)
        return jnp.where(even, own, other), jnp.where(even, other, own)

    def add(i, total):
        real, imag = load(i)
        square = real * real + imag * imag
        return total + square[:8] + square[8:]

    total = lax.fori_loop(0, groups // 2, add, jnp.zeros((8, wide), jnp.float32), unroll=groups // 2)
    same = (
        lax.broadcasted_iota(jnp.int32, (wide, wide), 0) // GROUP
        == lax.broadcasted_iota(jnp.int32, (wide, wide), 1) // GROUP
    ).astype(jnp.float32)
    terms, left_over = [], total
    for _ in range(3):
        terms.append(left_over.astype(jnp.bfloat16).astype(jnp.float32))
        left_over = left_over - terms[-1]
    power = jnp.dot(
        jnp.concatenate(terms, 0).astype(jnp.bfloat16),
        same.astype(jnp.bfloat16),
        preferred_element_type=jnp.float32,
    )
    power = power[:8] + power[8:16] + power[16:]
    scale = lax.rsqrt(power / freq_count + 1e-06)
    scale = jnp.concatenate([scale, scale], 0)

    def apply(i, carry):
        rows = pl.ds(pl.multiple_of(i * 16, 16), 16)
        for part, value in enumerate(load(i)):
            spec_ref[part, rows, :] = (value * scale).astype(jnp.bfloat16).astype(jnp.float32)
        return carry

    lax.fori_loop(0, groups // 2, apply, 0, unroll=groups // 2)

    diagonal = [
        lax.broadcasted_iota(jnp.int32, (8, wide), 1) % GROUP
        == lax.broadcasted_iota(jnp.int32, (8, wide), 0) + low
        for low in (0, 8)
    ]
    zero = jnp.zeros((8, wide), jnp.float32)

    def cross_of(group, carry):
        tiles = []
        for part in range(2):
            rows = spec_ref[part, pl.ds(pl.multiple_of(group * 8, 8), 8), :]
            for at in sources:
                row = jnp.broadcast_to(rows[at : at + 1, :], (8, wide))
                tiles += [jnp.where(mask, row, zero) for mask in diagonal]
        bins = pl.ds(pl.multiple_of(group * GROUP, GROUP), GROUP)
        real = receivers_ref[0, :, bins, :].reshape(wide, channels_here)
        imag = receivers_ref[1, :, bins, :].reshape(wide, channels_here)
        cross = jnp.dot(
            jnp.concatenate(tiles, 0).astype(jnp.bfloat16),
            jnp.concatenate([real, imag], 1),
            preferred_element_type=jnp.float32,
        )
        half = count * GROUP
        parts = (
            cross[:half, :channels_here] + cross[half:, channels_here:],
            cross[:half, channels_here:] - cross[half:, :channels_here],
        )
        for part, value in enumerate(parts):
            value = value.astype(jnp.bfloat16)
            rows = pl.ds(pl.multiple_of(part * freq_count + group * GROUP, GROUP), GROUP)
            for at in range(count):
                ref, pair = (cross_ref, at // 2) if at < done else (refs[0], (at - done) // 2)
                lanes = slice((at % 2) * channels_here, (at % 2 + 1) * channels_here)
                ref[pair, rows, lanes] = value[at * GROUP : (at + 1) * GROUP]
        return carry

    lax.fori_loop(0, groups, cross_of, 0, unroll=groups)
    transform(cross_ref, table_ref, out_ref)


def transform(cross_ref, table_ref, out_ref):
    channels_here = out_ref.shape[2]
    rows = 128
    for pair in range(cross_ref.shape[0]):
        for block in range(table_ref.shape[0] // rows):
            lags = slice(block * rows, (block + 1) * rows)
            value = jnp.dot(
                table_ref[lags, :], cross_ref[pair], preferred_element_type=jnp.float32
            ).astype(jnp.bfloat16)
            out_ref[2 * pair, lags, :] = value[:, :channels_here]
            out_ref[2 * pair + 1, lags, :] = value[:, channels_here:]


def lags_of(own, other, receivers, table, base, sources, done, hours, after):
    _, window_count, freq_count, channels_here = receivers.shape
    wide = own.shape[1]
    count = len(sources)
    cross = lambda some: (some // 2, 2 * freq_count, 2 * channels_here)
    out_shape = [jax.ShapeDtypeStruct((done, table.shape[0], channels_here), jnp.bfloat16)]
    if done < count:
        out_shape.append(jax.ShapeDtypeStruct(cross(count - done), jnp.bfloat16))
    return pl.pallas_call(
        functools.partial(lags_kernel, base, sources, done, hours),
        in_specs=[VMEM] * 4 + [ANY],
        out_specs=[VMEM] * len(out_shape),
        out_shape=out_shape,
        scratch_shapes=[
            pltpu.VMEM((2, freq_count // GROUP * 8, wide), jnp.float32),
            pltpu.VMEM(cross(done), jnp.bfloat16),
        ],
        compiler_params=pltpu.CompilerParams(vmem_limit_bytes=16 * MIB),
        cost_estimate=COST,
        name="lags",
    )(own, other, receivers, table, after)


def lags_of_rest(cross, table, after):
    pairs, _, lanes = cross.shape
    return pl.pallas_call(
        lambda cross_ref, table_ref, after_ref, out_ref: transform(cross_ref, table_ref, out_ref),
        in_specs=[VMEM, VMEM, ANY],
        out_specs=VMEM,
        out_shape=jax.ShapeDtypeStruct((2 * pairs, table.shape[0], lanes // 2), jnp.bfloat16),
        compiler_params=pltpu.CompilerParams(vmem_limit_bytes=16 * MIB),
        cost_estimate=COST,
        name="lags_rest",
    )(cross, table, after)


def sum_kernel(firsts, low, *refs):
    out_ref, rest = refs[len(firsts) + 1], refs[len(firsts) + 2 :]
    total_ref = rest[0] if rest else out_ref
    copies = []
    for source in range(low, low + out_ref.shape[0]):
        total = 0.0
        for first, ref in zip(firsts, refs):
            if first <= source < first + ref.shape[0]:
                total = total + ref[source - first].astype(jnp.float32)
        total_ref[source - low] = total.astype(total_ref.dtype)
        if rest and source % 2:
            pair = pl.ds(source - 1, 2)
            copies.append(
                pltpu.make_async_copy(total_ref.at[pair], out_ref.at[pair], rest[1].at[source // 2])
            )
            copies[-1].start()
    for copy in copies:
        copy.wait()


def sum_of(parts, low, high, dtype, after, final=False):
    firsts, values = zip(*parts)
    shape = (high - low,) + values[0].shape[1:]
    scratch = [pltpu.VMEM(shape, dtype), pltpu.SemaphoreType.DMA(((high - low) // 2,))]
    return pl.pallas_call(
        functools.partial(sum_kernel, firsts, low),
        in_specs=[VMEM] * len(values) + [ANY],
        out_specs=HBM if final else VMEM,
        out_shape=jax.ShapeDtypeStruct(shape, dtype),
        scratch_shapes=scratch if final else [],
        compiler_params=pltpu.CompilerParams(vmem_limit_bytes=16 * MIB),
        cost_estimate=COST,
        name="sum",
    )(*values, after)


def chip_stages(chan_count):
    bits = [1 << b for b in range(1, chan_count.bit_length() - 1)]
    turned = bits[1:] + bits[:1]
    return [
        [(i, i ^ (odd_bit if i % 2 else even_bit)) for i in range(chan_count)]
        for even_bit, odd_bit in zip(bits, turned)
    ]


def body(chan_count, spectra, quality, sources):
    freq_count = spectra.shape[2]
    stages = chip_stages(chan_count)
    cores = [(i, i ^ 1) for i in range(chan_count)]
    over_chan = lambda value, pairs: lax.ppermute(value, "chan", pairs)
    over_hour = lambda value, pairs: lax.ppermute(value, "hour", pairs)

    own, other, data, onehot, usable, flags = front(spectra, quality, sources)
    slot_rows = own.shape[0]
    state = {0: own}
    moved = {0: over_chan(other, cores)}
    passes = [0, 0, 0]
    made, mine, cross, middle, outward = {}, {}, {}, {}, {}
    inward = {}
    cuts = (0, SPLITS[0], 8)
    last = onehot
    for step in STEPS:
        kind, at = step[0], int(step[1:] or 0)
        if kind == "r":
            for pairs in (stages[:1], stages[1:], [cores])[passes[at]]:
                last = state[at] = add_after(last, state[at], moved[at])
                moved[at] = over_chan(last, pairs)
            passes[at] += 1
        elif kind == "q":
            state[1], state[2], *others, scale = pick_rest(data, onehot, usable, flags, slot_rows, last)
            moved.update({1 + chunk: over_chan(value, cores) for chunk, value in enumerate(others)})
            last = scale
        elif kind == "t":
            table = last = lag_table(freq_count, LAGS, last)
        elif kind == "w":
            receivers = last = whiten(data, scale, last)
        elif kind in "li" or step == "k0":
            chunk = min(at, 2)
            some, first, hours = range(8), SPLITS[at], (0, 1, 2, 3)
            if at == 0:
                some = {"l": range(first), "k": range(first, 8), "i": range(8)}[kind]
                first, hours = len(some), INNER if kind == "i" else ENDS
            base = slot_rows * (at - chunk)
            values = lags_of(state[chunk], moved[chunk], receivers, table, base, some, first, hours, last)
            last = mine[at, kind] = values[0]
            cross[at] = values[-1]
            if kind != "i" and at < 3:
                inward[at, kind] = over_hour(last, INWARD)
        elif kind == "k":
            last = mine[at, kind] = lags_of_rest(cross[at], table, last)
            inward[at, kind] = over_hour(last, INWARD)
        elif kind in "mn":
            which, low = ("l", 0) if kind == "m" else ("k", SPLITS[at])
            part = (0, mine[0, "i"]) if at == 0 else (low, mine[at, which])
            high = low + inward[at, which].shape[0]
            last = sum_of([part, (low, inward[at, which])], low, high, jnp.bfloat16, last)
            middle[at, which] = over_hour(last, MIDDLE)
        elif kind in "fg":
            which, part = ("l", 0) if kind == "f" else ("k", 1)
            parts = [(0, mine[2, "l"]), (cuts[part], middle[0, which])]
            last = sum_of(parts, cuts[part], cuts[part + 1], jnp.bfloat16, last)
            outward[which] = over_hour(last, OUTWARD)
        elif kind == "h":
            parts = [(0, mine[3, "l"]), (0, outward["l"]), (0, middle[1, "l"])]
            early = last = sum_of(parts, 0, cuts[1], jnp.float32, last)
        elif kind == "p":
            parts = [(0, early), (cuts[1], mine[3, "l"][cuts[1] :]), (cuts[1], outward["k"])]
            parts += [(SPLITS[1], middle[1, "k"])]
            last = sum_of(parts, 0, 8, jnp.float32, last)
    return sum_of([(0, last), (0, inward[2, "l"])], 0, 8, jnp.bfloat16, last, final=True)


def solution(mesh):
    placed = (P(None, "hour", None, "chan"), P("hour", "chan"), P())
    return jax.shard_map(
        functools.partial(body, mesh.shape["chan"]),
        mesh=mesh,
        in_specs=placed,
        out_specs=P("hour", None, "chan"),
        check_vma=False,
    )
```
